32 devices in a mesh: grp: 2 (over x), dev: 16 (over z, y, core).
Axes of the slice: x: 2, y: 2, z: 4, core: 2. Of those that a mesh axis runs over, the one named last changes fastest.
Arguments:
- state: float32 [2, 3, 16777216], P('grp', None, 'dev'), may hold values from -6 to 6
- courant: float32 [16777216], P('dev'), may hold values from 0.25 to 1
- remesh: float32 [128, 128], replicated, may hold values from -0.5 to 0.5
- shell_dest: int32 [32768, 1], P('dev'), may hold values from 0 to 15; in each aligned block of 2048 rows (0 to 2047, 2048 to 4095, ...) at most 256 rows name the same one
- shell_row: int32 [32768], P('dev'), may hold values from 0 to 8191
- return_dest: int32 [32768, 1], P('dev'), may hold values from 0 to 15; in each aligned block of 2048 rows (0 to 2047, 2048 to 4095, ...) at most 256 rows name the same one
- return_row: int32 [32768], P('dev'), may hold values from 0 to 8191
- return_block: int32 [32768], P('dev'), may hold values from 0 to 127
Outputs:
- fields: float32 [2, 3, 16777216], P('grp', None, 'dev')
The draws below stay inside these ranges and needn't reach their ends.
Inputs may be any that keep to these rules, and one draw needn't show every extreme that they name: `shell_dest`: among the rows of one device (2048 aligned rows) no brick is named more than 256 times, a bound that some block reaches. `return_dest`: among the rows of one brick (2048 aligned rows) no owner is named more than 256 times, a bound that some block reaches.
All inputs are finite; a program needn't handle non-finite values.
Results may differ from the reference program's by a relative error of at most 0.00027.
Values sent between devices are 32-bit elements; how exact they have to be, the bound alone decides.
A program may use at most 192 MiB of HBM per device.

```python
import math
import jax
import jax.numpy as jnp
import numpy as np
from jax import lax

NX = 512
NY = 256
NZ = 128
NI = 64
NK = 128
BRICKS = 16
CELLS = 16777216
NJ_DEV = 128
NJ = 2048
SHELL = 16
SB = 2048
CAP = 256
RPB = 8192


def with_ends(drawn, stream_key, smallest, largest):
    extent = drawn.shape
    place = [jax.random.randint(jax.random.fold_in(stream_key, axis), (), 0, extent[axis]) for axis in range(len(extent))]
    drawn = drawn.at[tuple(place)].set(smallest)
    longest = extent.index(max(extent))
    place[longest] = (place[longest] + 1) % extent[longest]
    return drawn.at[tuple(place)].set(largest)


def steps_of(rng, shape, pieces, least, largest):
    loudness = 1.0
    for axis_at, shards_of in pieces:
        heights = jax.random.uniform(jax.random.fold_in(jax.random.fold_in(rng, 6), axis_at), (shards_of,), jnp.float32, least / len(pieces), largest / len(pieces))
        loudness = loudness * jnp.repeat(jnp.exp(heights), shape[axis_at] // shards_of).reshape((-1,) + (1,) * (len(shape) - 1 - axis_at))
    return loudness


def assign_block(stream_key, own, number, rows, number_of, top, most, lean):
    order = jax.random.permutation(stream_key, number_of)
    packed, ordinary = shares(number_of, rows * top, most, lean, True), shares(number_of, rows * top, most, lean, False)
    places = jnp.arange(number_of)

    def named(sizes, turn):
        used = int((sizes > 0).sum())
        fixed = max(1, used // 4)
        moved = fixed + (places - fixed + turn * (used - fixed)) % max(1, number_of - fixed)
        return jnp.zeros((number_of,), jnp.int32).at[order[jnp.where(places < fixed, places, moved)]].set(jnp.asarray(sizes, jnp.int32))

    sizes = jnp.where(number % 4 == 0, named(packed, number // 4), named(ordinary, number - number // 4 - 1))
    mixed = jax.random.permutation(jax.random.fold_in(own, 3), number_of)
    donor, taker = mixed[0:number_of // 2 * 2:2], mixed[1:number_of // 2 * 2:2]
    margin = jnp.minimum(sizes[donor] - 1, most - sizes[taker]) // 2
    margin = jnp.where((donor == order[0]) | (taker == order[0]) | (sizes[taker] == 0), 0, jnp.maximum(margin, 0))
    moved = jax.random.randint(jax.random.fold_in(own, 4), (number_of // 2,), 0, 1 << 20) % (margin + 1)
    sizes = sizes.at[donor].add(-moved).at[taker].add(moved)
    items = jnp.searchsorted(jnp.cumsum(sizes), jnp.arange(rows * top), side="right").astype(jnp.int32)
    listing = items.reshape(top, rows).T
    listing = listing[jax.random.permutation(jax.random.fold_in(own, 1), rows)]
    turn = jax.random.randint(jax.random.fold_in(own, 2), (rows, 1), 0, top)
    return jnp.take_along_axis(listing, (jnp.arange(top)[None, :] + turn) % top, axis=1)


def shares(amount, total, most, skew, full):
    portions = [(1 << 20) // math.isqrt(rank ** skew) + 1 for rank in range(1, amount + 1)]
    largest = most if full else min(most, max(-(-total // amount), total * portions[0] // sum(portions)))
    least = 1 if total - largest >= amount - 1 else 0
    given, rest = [largest] + [least] * (amount - 1), total - largest - least * (amount - 1)
    while rest > 0:
        movable = [i for i in range(1, amount) if given[i] < largest] or [i for i in range(1, amount) if given[i] < most]
        mass, remaining = sum([portions[i] for i in movable]), rest
        for i in movable:
            more = min(most - given[i], max(1, remaining * portions[i] // mass), rest)
            given[i] = given[i] + more
            rest = rest - more
    return np.array(given)


def scatter_about(stream_key, shape, width, most, shards=(), kind=jnp.bfloat16):
    values = width * jax.random.normal(stream_key, shape, jnp.float32)
    if shards:
        values = values * steps_of(stream_key, shape, shards, -0.22, 0.18)
    return jnp.clip(values, -most, most).astype(kind)


def setup_inputs(seed: int = 0) -> dict:
    arg_keys = jax.random.split(jax.random.key(seed), 9)
    state = scatter_about(arg_keys[0], (2, 3, CELLS), 1.0, 6.0, ((0, 2), (2, 16)), jnp.float32)
    courant = jnp.clip(jnp.exp(math.log(1.0) - 1.3862944 * jax.random.uniform(arg_keys[1], (CELLS,), jnp.float32) ** steps_of(arg_keys[1], (CELLS,), ((0, 16),), -0.2, 0.2)), 0.25, 1.0)
    remesh = scatter_about(arg_keys[2], (NK, NZ), NK ** -0.5, 0.5, (), jnp.float32)
    shell_dest_keys = jax.random.split(jax.random.fold_in(arg_keys[3], 1), (BRICKS * SB) // SB)
    shell_dest_turns = jax.random.permutation(jax.random.fold_in(arg_keys[3], 3), (BRICKS * SB) // SB)
    shell_dest = jax.vmap(lambda own, number: assign_block(jax.random.fold_in(arg_keys[3], 2), own, number, SB, BRICKS, 1, CAP, 2))(shell_dest_keys, shell_dest_turns).reshape((BRICKS * SB, 1))
    shell_row = with_ends(jax.random.randint(arg_keys[4], (BRICKS * SB,), 0, RPB), jax.random.fold_in(arg_keys[4], 1), 0, RPB - 1).astype(jnp.int32)
    return_dest_keys = jax.random.split(jax.random.fold_in(arg_keys[5], 1), (BRICKS * SB) // SB)
    return_dest_turns = jax.random.permutation(jax.random.fold_in(arg_keys[5], 3), (BRICKS * SB) // SB)
    return_dest = jax.vmap(lambda own, number: assign_block(jax.random.fold_in(arg_keys[5], 2), own, number, SB, BRICKS, 1, CAP, 2))(return_dest_keys, return_dest_turns).reshape((BRICKS * SB, 1))
    return_row = with_ends(jax.random.randint(arg_keys[6], (BRICKS * SB,), 0, RPB), jax.random.fold_in(arg_keys[6], 1), 0, RPB - 1).astype(jnp.int32)
    return_block = with_ends(jax.random.randint(arg_keys[7], (BRICKS * SB,), 0, NJ_DEV), jax.random.fold_in(arg_keys[7], 1), 0, NJ_DEV - 1).astype(jnp.int32)
    return dict(state=state, courant=courant, remesh=remesh, shell_dest=shell_dest, shell_row=shell_row, return_dest=return_dest, return_row=return_row, return_block=return_block)


viscosity = 0.2
coupling = 1.0
highest = lax.Precision.HIGHEST


def sine_table(length):
    counts = jnp.arange(length, dtype=jnp.int32) + 1
    phase = (counts[:, None] * counts[None, :]) % (2 * (length + 1))
    return jnp.sin(jnp.pi * phase.astype(jnp.float32) / (length + 1))


def laplace_eigen(length):
    counts = jnp.arange(length, dtype=jnp.float32) + 1.0
    return 2.0 - 2.0 * jnp.cos(jnp.pi * counts / (length + 1))


def advance(field, courant_part):
    transport = (8.0 * (field[:, 3:-1] - field[:, 1:-3]) - (field[:, 4:] - field[:, :-4])) / 12.0
    centre_part = field[:, 2:-2]
    padded = jnp.pad(centre_part, ((0, 0), (0, 0), (1, 1), (0, 0)))
    diffusion = padded[:, :, 2:] - 2.0 * centre_part + padded[:, :, :-2]
    return centre_part - courant_part * transport + viscosity * diffusion


def difference(field, axis):
    widths = [(0, 0)] * field.ndim
    widths[axis] = (1, 1)
    padded = jnp.pad(field, widths)
    upper = lax.slice_in_dim(padded, 2, padded.shape[axis], axis=axis)
    lower = lax.slice_in_dim(padded, 0, padded.shape[axis] - 2, axis=axis)
    return (upper - lower) / 2.0


def cross_product(first, second):
    return jnp.stack([first[1] * second[2] - first[2] * second[1],
                      first[2] * second[0] - first[0] * second[2],
                      first[0] * second[1] - first[1] * second[0]])


def reference(state, courant, remesh, shell_dest, shell_row, return_dest, return_row, return_block):
    near_field = state[0].reshape(3, NJ, NI, NK)
    courant_field = courant.reshape(NJ, NI, NK)
    updated = near_field
    for substep in range(2):
        extended = jnp.concatenate([updated[:, -2:], updated, updated[:, :2]], axis=1)
        updated = advance(extended, courant_field)
    blocks = near_field[:, :, NI - SHELL:, :].reshape(3, NJ * SHELL, NK)
    remeshed = jnp.einsum('cqk,kz->cqz', blocks, remesh, precision=highest)
    lattice_rows = shell_dest[:, 0] * RPB + shell_row
    deposit = jnp.zeros((3, NX * NY, NZ), jnp.float32).at[:, lattice_rows, :].add(remeshed)
    wake_field = state[1].reshape(3, NX, NY, NZ) + deposit.reshape(3, NX, NY, NZ)
    spectral = jnp.einsum('cxyz,zb->cxyb', wake_field, sine_table(NZ), precision=highest)
    spectral = jnp.einsum('cxyb,ya->cxab', spectral, sine_table(NY), precision=highest)
    spectral = jnp.einsum('cxab,xe->ceab', spectral, sine_table(NX), precision=highest)
    eigen_sum = (laplace_eigen(NX)[:, None, None] + laplace_eigen(NY)[None, :, None]) + laplace_eigen(NZ)[None, None, :]
    scale = 8.0 / ((NX + 1) * (NY + 1) * (NZ + 1))
    spectral = spectral * (scale / eigen_sum)
    potential = jnp.einsum('ceab,ex->cxab', spectral, sine_table(NX), precision=highest)
    potential = jnp.einsum('cxab,ay->cxyb', potential, sine_table(NY), precision=highest)
    potential = jnp.einsum('cxyb,bz->cxyz', potential, sine_table(NZ), precision=highest)
    velocity = jnp.stack([difference(potential[2], 1) - difference(potential[1], 2),
                          difference(potential[0], 2) - difference(potential[2], 0),
                          difference(potential[1], 0) - difference(potential[0], 1)])
    flat_rows = velocity.reshape(3, NX * NY, NZ)
    brick_of = jnp.arange(BRICKS * SB, dtype=jnp.int32) // SB
    picked = jnp.take(flat_rows, brick_of * RPB + return_row, axis=1)
    interp = jnp.einsum('cqz,kz->cqk', picked, remesh, precision=highest)
    targets = return_dest[:, 0] * NJ_DEV + return_block
    boundary = jnp.zeros((3, NJ, NK), jnp.float32).at[:, targets, :].add(interp)
    updated = updated.at[:, :, NI - 1, :].add(coupling * cross_product(boundary, near_field[:, :, NI - 1, :]))
    return jnp.stack([updated.reshape(3, CELLS), velocity.reshape(3, CELLS)])
```

```python
import functools

import jax
import jax.numpy as jnp
import ml_dtypes
import numpy as np
from jax import lax
from jax.experimental import pallas as pl
from jax.experimental.pallas import tpu as pltpu
from jax.sharding import PartitionSpec as P

NX = 512
NY = 256
NI = 64

viscosity = 0.2
coupling = 1.0

VMEM = pl.BlockSpec(memory_space=pltpu.VMEM)
SMEM = pl.BlockSpec(memory_space=pltpu.SMEM)
HBM = pl.BlockSpec(memory_space=pl.ANY)
ROOM = pltpu.CompilerParams(vmem_limit_bytes=56 * 1024 * 1024)


def sine_table(length):
    counts = np.arange(length, dtype=np.int64) + 1
    phase = counts[:, None] * counts[None, :] % (2 * (length + 1))
    table = np.sin(np.pi * phase / (length + 1)).astype(np.float32)
    high = table.astype(ml_dtypes.bfloat16)
    low = (table - high.astype(np.float32)).astype(ml_dtypes.bfloat16)
    return np.stack([high, low])


def laplace_eigen(length):
    counts = np.arange(length, dtype=np.float64) + 1.0
    return 4.0 * np.sin(0.5 * np.pi * counts / (length + 1)) ** 2


def split(value):
    high = value.astype(jnp.bfloat16)
    return high, (value - high.astype(jnp.float32)).astype(jnp.bfloat16)


def dot_pairs(left, right):
    dot = functools.partial(jnp.dot, preferred_element_type=jnp.float32)
    return dot(left[0], right[0]) + (dot(left[0], right[1]) + dot(left[1], right[0]))


def power(base, exponent):
    result = None
    while exponent:
        if exponent & 1:
            result = base if result is None else result * base
        exponent >>= 1
        if exponent:
            base = base * base
    return result


def move(source, target, sem):
    copy = pltpu.make_async_copy(source, target, sem)
    copy.start()
    return copy


def loop(count, body):
    lax.fori_loop(0, count, lambda i, _: (body(i), 0)[1], 0)


def unrolled(count, width, body):
    while count % width:
        width //= 2

    def several(i):
        for t in range(width):
            body(i * width + t)

    loop(count // width, several)


def index_kernel(cap, stride, bricks, dest_a, tag_a, dest_b, tag_b, slot_a, slot_b, out):
    def clear(b):
        out[(2 * b) * stride + cap] = 0
        out[(2 * b + 1) * stride + cap] = 0

    loop(bricks, clear)

    def place(q):
        for side, (dest, tag, slot) in enumerate(((dest_a, tag_a, slot_a), (dest_b, tag_b, slot_b))):
            brick = dest[q]
            base = (2 * brick + side) * stride
            rank = out[base + cap]
            out[base + cap] = rank + 1
            slot[q] = brick * (3 * cap) + rank
            out[base + rank] = tag[q]

    unrolled(dest_a.shape[0], 8, place)


def pack_kernel(cap, group, slot, rows, out):
    @pl.when(lax.axis_index("grp") == group)
    def _():
        def place(i):
            first = pl.multiple_of(i * 8, 8)
            slots = [slot[first + t] for t in range(8)]
            for c in range(3):
                tile = rows[c, pl.ds(first, 8), :]
                for t in range(8):
                    out[pl.ds(slots[t] + c * cap, 1), :] = tile[t : t + 1, :]

        loop(rows.shape[1] // 8, place)


def accumulate(cap, stride, side, bricks, index, arrived, total):
    def from_brick(b):
        base = (2 * b + side) * stride

        def add(k):
            row = index[base + k]
            first = b * (3 * cap) + k
            news = [arrived[pl.ds(first + c * cap, 1), :] for c in range(3)]
            olds = [total[c, pl.ds(row, 1), :] for c in range(3)]
            for c in range(3):
                total[c, pl.ds(row, 1), :] = olds[c] + news[c]

        loop(index[base + cap], add)

    loop(bricks, from_brick)


def forward_kernel(
    cap, stride, bricks, index, arrived, field, decay, table_y, table_z, out, moments, held, sem
):
    planes = field.shape[1] // NY

    @pl.when(lax.axis_index("grp") == 1)
    def _():
        move(field, held, sem).wait()
        accumulate(cap, stride, 0, bricks, index, arrived, held)
        moments[...] = jnp.zeros_like(moments)
        r = decay[0]
        decay_now = (table_z[0], table_z[1])

        def plane(i):
            rows = pl.ds(pl.multiple_of(i * NY, NY), NY)
            parts = [dot_pairs(split(held[c, rows, :]), decay_now) for c in range(3)]
            wide = dot_pairs((table_y[0], table_y[1]), split(jnp.concatenate(parts, axis=1)))
            width = wide.shape[1] // 3
            for c in range(3):
                now = wide[:, c * width : (c + 1) * width]
                held[c, rows, :] = now
                moments[0, c] = now + r * moments[0, c]

        loop(planes, plane)
        sent = move(held, out, sem)

        def back(i):
            rows = pl.ds(pl.multiple_of((planes - 1 - i) * NY, NY), NY)
            for c in range(3):
                moments[1, c] = r * (held[c, rows, :] + moments[1, c])

        loop(planes, back)
        sent.wait()


def reduced_kernel(planes, moments, decay, out):
    bricks = moments.shape[0]
    r = decay[...]
    r_slab = power(r, planes)
    r_line = power(r, bricks * planes + 1)
    zero = jnp.zeros(moments.shape[2:], jnp.float32)

    def up(d, carry):
        out[d, 0] = carry
        return moments[d, 0] + r_slab * carry

    def down(i, carry):
        d = bricks - 1 - i
        out[d, 1] = carry
        return moments[d, 1] + r_slab * carry

    right = r * lax.fori_loop(0, bricks, up, zero)
    left = lax.fori_loop(0, bricks, down, zero)
    inverse = 1.0 / (1.0 - r_line * r_line)
    start = (right * r_line - left) * inverse
    end = (left * r_line - right) * inverse

    def add_up(d, carry):
        out[d, 0] += carry
        return r_slab * carry

    def add_down(i, carry):
        d = bricks - 1 - i
        out[d, 1] += carry
        return r_slab * carry

    lax.fori_loop(0, bricks, add_up, start)
    lax.fori_loop(0, bricks, add_down, r * end)


def backward_kernel(
    row, spectral, edges, decay, table_y, table_z, remesh_t, _fields, fields, interp, held, pot, run, sem
):
    planes = spectral.shape[1] // NY

    @pl.when(lax.axis_index("grp") == 1)
    def _():
        move(spectral, held, sem).wait()
        r = decay[0]
        gain = decay[1]
        run[...] = edges[...]

        def rows_of(i):
            return pl.ds(pl.multiple_of(i * NY, NY), NY)

        def potential(i, modes):
            wide = dot_pairs((table_y[0], table_y[1]), split(jnp.concatenate(modes, axis=1)))
            width = wide.shape[1] // 3
            for c in range(3):
                part = split(wide[:, c * width : (c + 1) * width])
                pot[c, rows_of(i), :] = dot_pairs(part, (table_z[0], table_z[1]))

        def back(i):
            at = planes - 1 - i
            for c in range(3):
                q = run[1, c]
                pot[c, rows_of(at + 1), :] = q
                run[1, c] = r * (held[c, rows_of(at), :] + q)

        loop(planes, back)
        potential(0, [gain * (run[0, c] + run[1, c]) for c in range(3)])

        def ahead(i):
            modes = []
            for c in range(3):
                p = held[c, rows_of(i), :] + r * run[0, c]
                run[0, c] = p
                modes.append(gain * (p + pot[c, rows_of(i + 1), :]))
            potential(i + 1, modes)

        loop(planes, ahead)
        potential(planes + 1, [gain * (r * run[0, c] + edges[1, c] / r) for c in range(3)])

        depth = pot.shape[2]
        y_at = lax.broadcasted_iota(jnp.int32, (NY, depth), 0)
        z_at = lax.broadcasted_iota(jnp.int32, (NY, depth), 1)

        def d_y(f):
            upper = jnp.where(y_at == NY - 1, 0.0, pltpu.roll(f, NY - 1, 0))
            return upper - jnp.where(y_at == 0, 0.0, pltpu.roll(f, 1, 0))

        def d_z(f):
            upper = jnp.where(z_at == depth - 1, 0.0, pltpu.roll(f, depth - 1, 1))
            return upper - jnp.where(z_at == 0, 0.0, pltpu.roll(f, 1, 1))

        def curl(i):
            here = rows_of(i + 1)
            f = [pot[c, here, :] for c in range(3)]
            slope_y = pot[1, rows_of(i + 2), :] - pot[1, rows_of(i), :]
            slope_z = pot[2, rows_of(i + 2), :] - pot[2, rows_of(i), :]
            held[0, rows_of(i), :] = 0.5 * (d_y(f[2]) - d_z(f[1]))
            held[1, rows_of(i), :] = 0.5 * (d_z(f[0]) - slope_z)
            held[2, rows_of(i), :] = 0.5 * (slope_y - d_y(f[0]))

        loop(planes, curl)
        sent = move(held, fields, sem)

        def pick(i):
            first = pl.multiple_of(i * 8, 8)
            places = [row[first + t] for t in range(8)]
            for c in range(3):
                for t in range(8):
                    interp[c, pl.ds(first + t, 1), :] = held[c, pl.ds(places[t], 1), :]

        loop(interp.shape[1] // 8, pick)
        weights = split(remesh_t[...])
        count = min(256, interp.shape[1])

        def project(i):
            rows = pl.ds(pl.multiple_of(i * count, count), count)
            for c in range(3):
                interp[c, rows, :] = dot_pairs(split(interp[c, rows, :]), weights)

        loop(interp.shape[1] // count, project)
        sent.wait()


def advance_kernel(near, courant, before, after, out, ext, first, sems):
    rows_j = near.shape[1]

    @pl.when(lax.axis_index("grp") == 0)
    def _():
        copies = [
            move(near, ext.at[pl.ds(0, 3), pl.ds(4, rows_j)], sems.at[0]),
            move(courant, ext.at[3, pl.ds(4, rows_j)], sems.at[1]),
            move(before, ext.at[:, pl.ds(0, 4)], sems.at[2]),
            move(after, ext.at[:, pl.ds(rows_j + 4, 4)], sems.at[3]),
        ]
        for copy in copies:
            copy.wait()
        i_at = lax.broadcasted_iota(jnp.int32, near.shape[2:], 0)

        def stepped(f, speed):
            transport = (8.0 * (f[3] - f[1]) - (f[4] - f[0])) * (1.0 / 12.0)
            upper = jnp.where(i_at == NI - 1, 0.0, pltpu.roll(f[2], NI - 1, 0))
            lower = jnp.where(i_at == 0, 0.0, pltpu.roll(f[2], 1, 0))
            return f[2] - speed * transport + viscosity * (upper - 2.0 * f[2] + lower)

        def one(j):
            speed = ext[3, j + 2]
            for c in range(3):
                first[c, j] = stepped([ext[c, j + t] for t in range(5)], speed)

        loop(rows_j + 4, one)

        def two(j):
            speed = ext[3, j + 4]
            for c in range(3):
                ext[c, j] = stepped([first[c, j + t] for t in range(5)], speed)

        loop(rows_j, two)
        move(ext.at[pl.ds(0, 3), pl.ds(0, rows_j)], out, sems.at[0]).wait()


def finish_kernel(cap, stride, bricks, index, arrived, layer, _fields, fields, boundary, rim, sem):
    @pl.when(lax.axis_index("grp") == 0)
    def _():
        fetched = move(fields.at[:, :, pl.ds(NI - 8, 8), :], rim, sem)
        boundary[...] = jnp.zeros_like(boundary)
        accumulate(cap, stride, 1, bricks, index, arrived, boundary)
        fetched.wait()
        for c in range(3):
            a, b = (c + 1) % 3, (c + 2) % 3
            turned = coupling * (boundary[a] * layer[b] - boundary[b] * layer[a])
            rim[c, :, 7, :] += turned
        move(rim, fields.at[:, :, pl.ds(NI - 8, 8), :], sem).wait()


def on_device(state, courant, remesh, shell_dest, shell_row, return_dest, return_row, return_block):
    bricks = lax.axis_size("dev")
    cell_count = state.shape[2]
    span_cells, lattice_z = remesh.shape
    rows_j = cell_count // (NI * span_cells)
    shell_depth = NI // 4
    shell_blocks = shell_depth * rows_j
    cap = 2 * shell_blocks // bricks
    stride = -(-(cap + 1) // 128) * 128
    planes = NX // bricks
    slab_rows = planes * NY
    f32 = functools.partial(jax.ShapeDtypeStruct, dtype=jnp.float32)
    i32 = functools.partial(jax.ShapeDtypeStruct, dtype=jnp.int32)
    field = state[0].reshape(3, slab_rows, lattice_z)
    near = field.reshape(3, rows_j, NI, span_cells)

    blocks = near[:, :, NI - shell_depth :, :].reshape(3, shell_blocks, span_cells)
    remeshed = jnp.einsum("cqk,kz->cqz", blocks, remesh, precision=lax.Precision.HIGH)
    crossed = lax.ppermute(remeshed, "grp", [(0, 1)])

    slot_shell, slot_back, tags = pl.pallas_call(
        functools.partial(index_kernel, cap, stride, bricks),
        out_shape=(i32((shell_blocks,)), i32((shell_blocks,)), i32((bricks * 2 * stride,))),
        in_specs=[SMEM] * 4,
        out_specs=(SMEM,) * 3,
    )(shell_dest[:, 0], shell_row, return_dest[:, 0], return_block)
    index = lax.all_to_all(
        tags.reshape(bricks, 2 * stride), "dev", split_axis=0, concat_axis=0, tiled=True
    ).reshape(-1)

    def exchange(rows, slots, group):
        packed = pl.pallas_call(
            functools.partial(pack_kernel, cap, group),
            out_shape=f32((bricks * 3 * cap, lattice_z)),
            in_specs=[SMEM, VMEM],
            out_specs=VMEM,
            compiler_params=ROOM,
        )(slots, rows)
        return lax.all_to_all(
            packed.reshape(bricks, 3 * cap, lattice_z),
            "dev",
            split_axis=0,
            concat_axis=0,
            tiled=True,
        ).reshape(bricks * 3 * cap, lattice_z)

    arrived = exchange(crossed, slot_shell, 1)

    table_y = sine_table(NY)
    table_z = sine_table(lattice_z)
    total = laplace_eigen(NY)[:, None] + laplace_eigen(lattice_z)[None, :]
    root = np.sqrt(total * (total + 4.0))
    decay = 2.0 / (2.0 + total + root)
    scale = 4.0 / ((NY + 1) * (lattice_z + 1))
    factors = jnp.asarray(np.stack([decay, scale / root]), jnp.float32)

    spectral, moments = pl.pallas_call(
        functools.partial(forward_kernel, cap, stride, bricks),
        out_shape=(f32((3, slab_rows, lattice_z)), f32((2, 3, NY, lattice_z))),
        in_specs=[SMEM, VMEM, HBM, VMEM, VMEM, VMEM],
        out_specs=(HBM, VMEM),
        scratch_shapes=[pltpu.VMEM((3, slab_rows, lattice_z), jnp.float32), pltpu.SemaphoreType.DMA],
        compiler_params=ROOM,
    )(index, arrived, field, factors, table_y, table_z)

    courant_near = courant.reshape(rows_j, NI, span_cells)
    ring_up = [(i, (i + 1) % bricks) for i in range(bricks)]
    ring_down = [(j, i) for i, j in ring_up]
    tail = jnp.concatenate([near[:, -4:], courant_near[None, -4:]], axis=0)
    head = jnp.concatenate([near[:, :4], courant_near[None, :4]], axis=0)
    before = lax.ppermute(tail, "dev", ring_up)
    after = lax.ppermute(head, "dev", ring_down)
    before, _ = lax.optimization_barrier((before, arrived))
    advanced = pl.pallas_call(
        advance_kernel,
        out_shape=f32((3, rows_j, NI, span_cells)),
        in_specs=[HBM] * 4,
        out_specs=HBM,
        scratch_shapes=[
            pltpu.VMEM((4, rows_j + 8, NI, span_cells), jnp.float32),
            pltpu.VMEM((3, rows_j + 4, NI, span_cells), jnp.float32),
            pltpu.SemaphoreType.DMA((4,)),
        ],
        compiler_params=ROOM,
    )(near, courant_near, before, after)

    lines = NY // bricks
    swapped = lax.all_to_all(
        moments.reshape(2, 3, bricks, lines, lattice_z).transpose(2, 0, 1, 3, 4),
        "dev",
        split_axis=0,
        concat_axis=0,
        tiled=True,
    )
    mine = lax.dynamic_slice_in_dim(factors[0], lax.axis_index("dev") * lines, lines)
    solved = pl.pallas_call(
        functools.partial(reduced_kernel, planes),
        out_shape=f32(swapped.shape),
        in_specs=[VMEM, VMEM],
        out_specs=VMEM,
    )(swapped, mine)
    edges = lax.all_to_all(solved, "dev", split_axis=0, concat_axis=0, tiled=True)
    edges = edges.transpose(1, 2, 0, 3, 4).reshape(2, 3, NY, lattice_z)

    fields, interp = pl.pallas_call(
        backward_kernel,
        out_shape=(f32((3, slab_rows, lattice_z)), f32((3, shell_blocks, span_cells))),
        in_specs=[SMEM, HBM, VMEM, VMEM, VMEM, VMEM, VMEM, HBM],
        out_specs=(HBM, VMEM),
        scratch_shapes=[
            pltpu.VMEM((3, slab_rows, lattice_z), jnp.float32),
            pltpu.VMEM((3, slab_rows + 2 * NY, lattice_z), jnp.float32),
            pltpu.VMEM((2, 3, NY, lattice_z), jnp.float32),
            pltpu.SemaphoreType.DMA,
        ],
        input_output_aliases={7: 0},
        compiler_params=ROOM,
    )(
        return_row,
        spectral,
        edges,
        factors,
        table_y,
        table_z,
        remesh.T,
        advanced.reshape(3, slab_rows, lattice_z),
    )

    returned = exchange(lax.ppermute(interp, "grp", [(1, 0)]), slot_back, 0)
    fields = pl.pallas_call(
        functools.partial(finish_kernel, cap, stride, bricks),
        out_shape=f32((3, rows_j, NI, span_cells)),
        in_specs=[SMEM, VMEM, VMEM, HBM],
        out_specs=HBM,
        scratch_shapes=[
            pltpu.VMEM((3, rows_j, span_cells), jnp.float32),
            pltpu.VMEM((3, rows_j, 8, span_cells), jnp.float32),
            pltpu.SemaphoreType.DMA,
        ],
        input_output_aliases={3: 0},
        compiler_params=ROOM,
    )(index, returned, near[:, :, NI - 1, :], fields.reshape(3, rows_j, NI, span_cells))
    return fields.reshape(1, 3, cell_count)


def solution(mesh):
    placed = (
        P("grp", None, "dev"),
        P("dev"),
        P(),
        P("dev", None),
        P("dev"),
        P("dev", None),
        P("dev"),
        P("dev"),
    )
    return jax.shard_map(
        on_device, mesh=mesh, in_specs=placed, out_specs=P("grp", None, "dev"), check_vma=False
    )
```

```python
import functools

import jax
import jax.numpy as jnp
import ml_dtypes
import numpy as np
from jax import lax
from jax.experimental import pallas as pl
from jax.experimental.pallas import tpu as pltpu
from jax.sharding import PartitionSpec as P

NX = 512
NY = 256
NI = 64

viscosity = 0.2
coupling = 1.0

VMEM = pl.BlockSpec(memory_space=pltpu.VMEM)
SMEM = pl.BlockSpec(memory_space=pltpu.SMEM)
HBM = pl.BlockSpec(memory_space=pl.ANY)
ROOM = pltpu.CompilerParams(vmem_limit_bytes=56 * 1024 * 1024)


def sine_table(length):
    counts = np.arange(length, dtype=np.int64) + 1
    phase = counts[:, None] * counts[None, :] % (2 * (length + 1))
    table = np.sin(np.pi * phase / (length + 1)).astype(np.float32)
    high = table.astype(ml_dtypes.bfloat16)
    low = (table - high.astype(np.float32)).astype(ml_dtypes.bfloat16)
    return np.stack([high, low])


def laplace_eigen(length):
    counts = np.arange(length, dtype=np.float64) + 1.0
    return 4.0 * np.sin(0.5 * np.pi * counts / (length + 1)) ** 2


def split(value):
    high = value.astype(jnp.bfloat16)
    return high, (value - high.astype(jnp.float32)).astype(jnp.bfloat16)


def dot_pairs(left, right):
    dot = functools.partial(jnp.dot, preferred_element_type=jnp.float32)
    return dot(left[0], right[0]) + (dot(left[0], right[1]) + dot(left[1], right[0]))


def doubled(pair):
    wide = jnp.concatenate(pair, axis=1)
    return jnp.concatenate([wide, wide], axis=0)


def dot_doubled(left, right):
    product = jnp.dot(
        jnp.concatenate(split(left), axis=1), right, preferred_element_type=jnp.float32
    )
    width = product.shape[1] // 2
    return product[:, :width] + product[:, width:]


def power(base, exponent):
    result = None
    while exponent:
        if exponent & 1:
            result = base if result is None else result * base
        exponent >>= 1
        if exponent:
            base = base * base
    return result


def move(source, target, sem):
    copy = pltpu.make_async_copy(source, target, sem)
    copy.start()
    return copy


def loop(count, body):
    lax.fori_loop(0, count, lambda i, _: (body(i), 0)[1], 0)


def unrolled(count, width, body):
    while count % width:
        width //= 2

    def several(i):
        for t in range(width):
            body(i * width + t)

    loop(count // width, several)


def index_kernel(cap, stride, bricks, dest_a, tag_a, dest_b, tag_b, slot_a, slot_b, out_a, out_b):
    half = dest_a.shape[0] // 2

    def clear(b):
        for out in (out_a, out_b):
            for end in range(2):
                out[b * stride + cap + end] = 0

    loop(bricks, clear)
    sides = ((dest_a, tag_a, slot_a, out_a), (dest_b, tag_b, slot_b, out_b))
    chains = [(side, end) for side in range(2) for end in range(2)]

    def place(q):
        at = [q + end * half for side, end in chains]
        brick = [sides[side][0][at[n]] for n, (side, end) in enumerate(chains)]
        tag = [sides[side][1][at[n]] for n, (side, end) in enumerate(chains)]
        base = [value * stride for value in brick]
        taken = [sides[side][3][base[n] + cap + end] for n, (side, end) in enumerate(chains)]
        for n, (side, end) in enumerate(chains):
            out = sides[side][3]
            rank = cap - 1 - taken[n] if end else taken[n]
            out[base[n] + cap + end] = taken[n] + 1
            out[base[n] + rank] = tag[n]
            sides[side][2][at[n]] = brick[n] * (3 * cap) + rank

    unrolled(half, 4, place)


def exchange_kernel(source, bricks, packed, tags, out, out_tags, send_sems, recv_sems):
    grp = lax.axis_index("grp")
    me = lax.axis_index("dev")
    barrier = pltpu.get_barrier_semaphore()

    def greet(i):
        pl.semaphore_signal(
            barrier,
            inc=1,
            device_id=(1 - grp, lax.rem(me + i, bricks)),
            device_id_type=pl.DeviceIdType.MESH,
        )

    loop(bricks, greet)
    pl.semaphore_wait(barrier, bricks)

    def copies(block, place, peer):
        return [
            pltpu.make_async_remote_copy(
                src_ref=source_ref.at[block],
                dst_ref=target_ref.at[place],
                send_sem=send_sems.at[n, block],
                recv_sem=recv_sems.at[n, place],
                device_id=(1 - grp, peer),
                device_id_type=pl.DeviceIdType.MESH,
            )
            for n, (source_ref, target_ref) in enumerate(((packed, out), (tags, out_tags)))
        ]

    @pl.when(grp == source)
    def _():
        def start(i):
            peer = lax.rem(me + i, bricks)
            for copy in copies(peer, me, peer):
                copy.start()

        def finish(peer):
            for copy in copies(peer, me, peer):
                copy.wait_send()

        loop(bricks, start)
        loop(bricks, finish)

    @pl.when(grp != source)
    def _():
        def finish(peer):
            for copy in copies(peer, peer, peer):
                copy.wait_recv()

        loop(bricks, finish)


def pack_kernel(cap, group, slot, rows, out):
    @pl.when(lax.axis_index("grp") == group)
    def _():
        def place(i):
            first = pl.multiple_of(i * 8, 8)
            slots = [slot[first + t] for t in range(8)]
            for c in range(3):
                tile = rows[c, pl.ds(first, 8), :]
                for t in range(8):
                    out[pl.ds(slots[t] + c * cap, 1), :] = tile[t : t + 1, :]

        loop(rows.shape[1] // 8, place)


def accumulate(cap, stride, bricks, index, arrived, total):
    def from_brick(b):
        base = b * stride

        def add(k):
            row = index[base + k]
            first = b * (3 * cap) + k
            news = [arrived[pl.ds(first + c * cap, 1), :] for c in range(3)]
            olds = [total[c, pl.ds(row, 1), :] for c in range(3)]
            for c in range(3):
                total[c, pl.ds(row, 1), :] = olds[c] + news[c]

        loop(index[base + cap], add)
        last = cap - 1
        loop(index[base + cap + 1], lambda k: add(last - k))

    loop(bricks, from_brick)


def forward_kernel(
    cap, stride, bricks, index, arrived, field, decay, table_y, table_z, out, moments, held, sem
):
    planes = field.shape[1] // NY

    @pl.when(lax.axis_index("grp") == 1)
    def _():
        move(field, held, sem).wait()
        accumulate(cap, stride, bricks, index, arrived, held)
        moments[...] = jnp.zeros_like(moments)
        r = decay[0]
        step = 2 - planes % 2

        def plane(i):
            first = i * (step * NY)
            rows = pl.ds(pl.multiple_of(first, NY), step * NY)
            parts = [dot_doubled(held[c, rows, :], table_z[...]) for c in range(3)]
            parts = [part[t * NY : (t + 1) * NY] for t in range(step) for part in parts]
            wide = dot_pairs((table_y[0], table_y[1]), split(jnp.concatenate(parts, axis=1)))
            width = wide.shape[1] // (3 * step)
            for c in range(3):
                total = moments[0, c]
                for t in range(step):
                    n = 3 * t + c
                    now = wide[:, n * width : (n + 1) * width]
                    held[c, pl.ds(pl.multiple_of(first + t * NY, NY), NY), :] = now
                    total = now + r * total
                moments[0, c] = total

        loop(planes // step, plane)
        sent = move(held, out, sem)

        def back(i):
            rows = pl.ds(pl.multiple_of((planes - 1 - i) * NY, NY), NY)
            for c in range(3):
                moments[1, c] = r * (held[c, rows, :] + moments[1, c])

        loop(planes, back)
        sent.wait()


def reduced_kernel(planes, moments, decay, out):
    bricks = moments.shape[0]
    r = decay[...]
    r_slab = power(r, planes)
    r_line = power(r, bricks * planes + 1)
    zero = jnp.zeros(moments.shape[2:], jnp.float32)

    def up(d, carry):
        out[d, 0] = carry
        return moments[d, 0] + r_slab * carry

    def down(i, carry):
        d = bricks - 1 - i
        out[d, 1] = carry
        return moments[d, 1] + r_slab * carry

    right = r * lax.fori_loop(0, bricks, up, zero)
    left = lax.fori_loop(0, bricks, down, zero)
    inverse = 1.0 / (1.0 - r_line * r_line)
    start = (right * r_line - left) * inverse
    end = (left * r_line - right) * inverse

    def add_up(d, carry):
        out[d, 0] += carry
        return r_slab * carry

    def add_down(i, carry):
        d = bricks - 1 - i
        out[d, 1] += carry
        return r_slab * carry

    lax.fori_loop(0, bricks, add_up, start)
    lax.fori_loop(0, bricks, add_down, r * end)


def backward_kernel(
    row, spectral, edges, decay, table_y, table_z, remesh_t, _fields, fields, interp, held, pot, run, sem
):
    planes = spectral.shape[1] // NY

    @pl.when(lax.axis_index("grp") == 1)
    def _():
        move(spectral, held, sem).wait()
        r = decay[0]
        gain = decay[1]
        run[...] = edges[...]

        def rows_of(i):
            return pl.ds(pl.multiple_of(i * NY, NY), NY)

        def potential(places, modes):
            wide = dot_pairs((table_y[0], table_y[1]), split(jnp.concatenate(modes, axis=1)))
            width = wide.shape[1] // len(modes)
            parts = [wide[:, n * width : (n + 1) * width] for n in range(len(modes))]
            for c in range(3):
                tall = dot_doubled(jnp.concatenate(parts[c::3], axis=0), table_z[...])
                for t, place in enumerate(places):
                    pot[c, rows_of(place), :] = tall[t * NY : (t + 1) * NY]

        def back(i):
            at = planes - 1 - i
            for c in range(3):
                q = run[1, c]
                pot[c, rows_of(at + 1), :] = q
                run[1, c] = r * (held[c, rows_of(at), :] + q)

        loop(planes, back)
        step = 2 - planes % 2

        def ahead(i):
            modes = []
            for t in range(step):
                at = i * step + t
                for c in range(3):
                    p = held[c, rows_of(at), :] + r * run[0, c]
                    run[0, c] = p
                    modes.append(gain * (p + pot[c, rows_of(at + 1), :]))
            potential([i * step + t + 1 for t in range(step)], modes)

        loop(planes // step, ahead)
        below = [gain * (edges[0, c] + run[1, c]) for c in range(3)]
        above = [gain * (r * run[0, c] + edges[1, c] / r) for c in range(3)]
        potential([0, planes + 1], below + above)

        depth = pot.shape[2]
        y_at = lax.broadcasted_iota(jnp.int32, (NY, depth), 0)
        z_at = lax.broadcasted_iota(jnp.int32, (NY, depth), 1)

        def d_y(f):
            upper = jnp.where(y_at == NY - 1, 0.0, pltpu.roll(f, NY - 1, 0))
            return upper - jnp.where(y_at == 0, 0.0, pltpu.roll(f, 1, 0))

        def d_z(f):
            upper = jnp.where(z_at == depth - 1, 0.0, pltpu.roll(f, depth - 1, 1))
            return upper - jnp.where(z_at == 0, 0.0, pltpu.roll(f, 1, 1))

        def curl(i):
            here = rows_of(i + 1)
            f = [pot[c, here, :] for c in range(3)]
            slope_y = pot[1, rows_of(i + 2), :] - pot[1, rows_of(i), :]
            slope_z = pot[2, rows_of(i + 2), :] - pot[2, rows_of(i), :]
            held[0, rows_of(i), :] = 0.5 * (d_y(f[2]) - d_z(f[1]))
            held[1, rows_of(i), :] = 0.5 * (d_z(f[0]) - slope_z)
            held[2, rows_of(i), :] = 0.5 * (slope_y - d_y(f[0]))

        loop(planes, curl)
        sent = move(held, fields, sem)

        def pick(i):
            first = pl.multiple_of(i * 8, 8)
            places = [row[first + t] for t in range(8)]
            for c in range(3):
                for t in range(8):
                    interp[c, pl.ds(first + t, 1), :] = held[c, pl.ds(places[t], 1), :]

        loop(interp.shape[1] // 8, pick)
        weights = doubled(split(remesh_t[...]))
        count = min(256, interp.shape[1])

        def project(i):
            rows = pl.ds(pl.multiple_of(i * count, count), count)
            for c in range(3):
                interp[c, rows, :] = dot_doubled(interp[c, rows, :], weights)

        loop(interp.shape[1] // count, project)
        sent.wait()


def advance_kernel(near, courant, before, after, out, ext, first, sems):
    rows_j = near.shape[1]

    @pl.when(lax.axis_index("grp") == 0)
    def _():
        copies = [
            move(near, ext.at[pl.ds(0, 3), pl.ds(4, rows_j)], sems.at[0]),
            move(courant, ext.at[3, pl.ds(4, rows_j)], sems.at[1]),
            move(before, ext.at[:, pl.ds(0, 4)], sems.at[2]),
            move(after, ext.at[:, pl.ds(rows_j + 4, 4)], sems.at[3]),
        ]
        for copy in copies:
            copy.wait()
        i_at = lax.broadcasted_iota(jnp.int32, near.shape[2:], 0)

        def stepped(f, speed):
            transport = (8.0 * (f[3] - f[1]) - (f[4] - f[0])) * (1.0 / 12.0)
            upper = jnp.where(i_at == NI - 1, 0.0, pltpu.roll(f[2], NI - 1, 0))
            lower = jnp.where(i_at == 0, 0.0, pltpu.roll(f[2], 1, 0))
            return f[2] - speed * transport + viscosity * (upper - 2.0 * f[2] + lower)

        def one(j):
            speed = ext[3, j + 2]
            for c in range(3):
                first[c, j] = stepped([ext[c, j + t] for t in range(5)], speed)

        loop(rows_j + 4, one)

        def two(j):
            speed = ext[3, j + 4]
            for c in range(3):
                ext[c, j] = stepped([first[c, j + t] for t in range(5)], speed)

        loop(rows_j, two)
        move(ext.at[pl.ds(0, 3), pl.ds(0, rows_j)], out, sems.at[0]).wait()


def finish_kernel(cap, stride, bricks, index, arrived, layer, _fields, fields, boundary, rim, sem):
    @pl.when(lax.axis_index("grp") == 0)
    def _():
        fetched = move(fields.at[:, :, pl.ds(NI - 8, 8), :], rim, sem)
        boundary[...] = jnp.zeros_like(boundary)
        accumulate(cap, stride, bricks, index, arrived, boundary)
        fetched.wait()
        for c in range(3):
            a, b = (c + 1) % 3, (c + 2) % 3
            turned = coupling * (boundary[a] * layer[b] - boundary[b] * layer[a])
            rim[c, :, 7, :] += turned
        move(rim, fields.at[:, :, pl.ds(NI - 8, 8), :], sem).wait()


def on_device(state, courant, remesh, shell_dest, shell_row, return_dest, return_row, return_block):
    bricks = lax.axis_size("dev")
    cell_count = state.shape[2]
    span_cells, lattice_z = remesh.shape
    rows_j = cell_count // (NI * span_cells)
    shell_depth = NI // 4
    shell_blocks = shell_depth * rows_j
    cap = 2 * shell_blocks // bricks
    stride = -(-(cap + 2) // 128) * 128
    planes = NX // bricks
    slab_rows = planes * NY
    f32 = functools.partial(jax.ShapeDtypeStruct, dtype=jnp.float32)
    i32 = functools.partial(jax.ShapeDtypeStruct, dtype=jnp.int32)
    field = state[0].reshape(3, slab_rows, lattice_z)
    near = field.reshape(3, rows_j, NI, span_cells)

    blocks = near[:, :, NI - shell_depth :, :].reshape(3, shell_blocks, span_cells)
    remeshed = jnp.einsum("cqk,kz->cqz", blocks, remesh, precision=lax.Precision.HIGH)

    courant_near = courant.reshape(rows_j, NI, span_cells)
    ring_up = [(i, (i + 1) % bricks) for i in range(bricks)]
    ring_down = [(j, i) for i, j in ring_up]
    tail = jnp.concatenate([near[:, -4:], courant_near[None, -4:]], axis=0)
    head = jnp.concatenate([near[:, :4], courant_near[None, :4]], axis=0)
    before = lax.ppermute(tail, "dev", ring_up)
    after = lax.ppermute(head, "dev", ring_down)

    slot_shell, slot_back, tags_shell, tags_back = pl.pallas_call(
        functools.partial(index_kernel, cap, stride, bricks),
        out_shape=(i32((shell_blocks,)), i32((shell_blocks,)), i32((bricks * stride,)), i32((bricks * stride,))),
        in_specs=[SMEM] * 4,
        out_specs=(SMEM,) * 4,
    )(shell_dest[:, 0], shell_row, return_dest[:, 0], return_block)
    def pack(rows, slots, group):
        return pl.pallas_call(
            functools.partial(pack_kernel, cap, group),
            out_shape=f32((bricks * 3 * cap, lattice_z)),
            in_specs=[SMEM, VMEM],
            out_specs=VMEM,
            compiler_params=ROOM,
        )(slots, rows).reshape(bricks, 3 * cap, lattice_z)

    def exchange(packed, tags, group):
        arrived, index = pl.pallas_call(
            functools.partial(exchange_kernel, group, bricks),
            out_shape=(f32((bricks, 3 * cap, lattice_z)), i32((bricks, stride // 128, 128))),
            in_specs=[HBM] * 2,
            out_specs=(HBM,) * 2,
            scratch_shapes=[pltpu.SemaphoreType.DMA((2, bricks))] * 2,
            compiler_params=pltpu.CompilerParams(collective_id=group, has_side_effects=True),
        )(packed, tags.reshape(bricks, stride // 128, 128))
        return arrived.reshape(bricks * 3 * cap, lattice_z), index.reshape(-1)

    packed = pack(remeshed, slot_shell, 0)
    packed, before, after = lax.optimization_barrier((packed, before, after))
    arrived, index = exchange(packed, tags_shell, 0)
    before, _ = lax.optimization_barrier((before, arrived))

    table_y = sine_table(NY)
    table_z = np.tile(np.concatenate(list(sine_table(lattice_z)), axis=1), (2, 1))
    total = laplace_eigen(NY)[:, None] + laplace_eigen(lattice_z)[None, :]
    root = np.sqrt(total * (total + 4.0))
    decay = 2.0 / (2.0 + total + root)
    scale = 4.0 / ((NY + 1) * (lattice_z + 1))
    factors = jnp.asarray(np.stack([decay, scale / root]), jnp.float32)

    spectral, moments = pl.pallas_call(
        functools.partial(forward_kernel, cap, stride, bricks),
        out_shape=(f32((3, slab_rows, lattice_z)), f32((2, 3, NY, lattice_z))),
        in_specs=[SMEM, VMEM, HBM, VMEM, VMEM, VMEM],
        out_specs=(HBM, VMEM),
        scratch_shapes=[pltpu.VMEM((3, slab_rows, lattice_z), jnp.float32), pltpu.SemaphoreType.DMA],
        compiler_params=ROOM,
    )(index, arrived, field, factors, table_y, table_z)

    advanced = pl.pallas_call(
        advance_kernel,
        out_shape=f32((3, rows_j, NI, span_cells)),
        in_specs=[HBM] * 4,
        out_specs=HBM,
        scratch_shapes=[
            pltpu.VMEM((4, rows_j + 8, NI, span_cells), jnp.float32),
            pltpu.VMEM((3, rows_j + 4, NI, span_cells), jnp.float32),
            pltpu.SemaphoreType.DMA((4,)),
        ],
        compiler_params=ROOM,
    )(near, courant_near, before, after)

    lines = NY // bricks
    swapped = lax.all_to_all(
        moments.reshape(2, 3, bricks, lines, lattice_z).transpose(2, 0, 1, 3, 4),
        "dev",
        split_axis=0,
        concat_axis=0,
        tiled=True,
    )
    mine = lax.dynamic_slice_in_dim(factors[0], lax.axis_index("dev") * lines, lines)
    solved = pl.pallas_call(
        functools.partial(reduced_kernel, planes),
        out_shape=f32(swapped.shape),
        in_specs=[VMEM, VMEM],
        out_specs=VMEM,
    )(swapped, mine)
    edges = lax.all_to_all(solved, "dev", split_axis=0, concat_axis=0, tiled=True)
    edges = edges.transpose(1, 2, 0, 3, 4).reshape(2, 3, NY, lattice_z)

    fields, interp = pl.pallas_call(
        backward_kernel,
        out_shape=(f32((3, slab_rows, lattice_z)), f32((3, shell_blocks, span_cells))),
        in_specs=[SMEM, HBM, VMEM, VMEM, VMEM, VMEM, VMEM, HBM],
        out_specs=(HBM, VMEM),
        scratch_shapes=[
            pltpu.VMEM((3, slab_rows, lattice_z), jnp.float32),
            pltpu.VMEM((3, slab_rows + 2 * NY, lattice_z), jnp.float32),
            pltpu.VMEM((2, 3, NY, lattice_z), jnp.float32),
            pltpu.SemaphoreType.DMA,
        ],
        input_output_aliases={7: 0},
        compiler_params=ROOM,
    )(
        return_row,
        spectral,
        edges,
        factors,
        table_y,
        table_z,
        remesh.T,
        advanced.reshape(3, slab_rows, lattice_z),
    )

    returned, index_back = exchange(pack(interp, slot_back, 1), tags_back, 1)
    fields = pl.pallas_call(
        functools.partial(finish_kernel, cap, stride, bricks),
        out_shape=f32((3, rows_j, NI, span_cells)),
        in_specs=[SMEM, VMEM, VMEM, HBM],
        out_specs=HBM,
        scratch_shapes=[
            pltpu.VMEM((3, rows_j, span_cells), jnp.float32),
            pltpu.VMEM((3, rows_j, 8, span_cells), jnp.float32),
            pltpu.SemaphoreType.DMA,
        ],
        input_output_aliases={3: 0},
        compiler_params=ROOM,
    )(index_back, returned, near[:, :, NI - 1, :], fields.reshape(3, rows_j, NI, span_cells))
    return fields.reshape(1, 3, cell_count)


def solution(mesh):
    placed = (
        P("grp", None, "dev"),
        P("dev"),
        P(),
        P("dev", None),
        P("dev"),
        P("dev", None),
        P("dev"),
        P("dev"),
    )
    return jax.shard_map(
        on_device, mesh=mesh, in_specs=placed, out_specs=P("grp", None, "dev"), check_vma=False
    )
```

```python
import functools

import jax
import jax.numpy as jnp
import ml_dtypes
import numpy as np
from jax import lax
from jax.experimental import pallas as pl
from jax.experimental.pallas import tpu as pltpu
from jax.sharding import PartitionSpec as P

NX = 512
NY = 256
NI = 64

viscosity = 0.2
coupling = 1.0

VMEM = pl.BlockSpec(memory_space=pltpu.VMEM)
SMEM = pl.BlockSpec(memory_space=pltpu.SMEM)
HBM = pl.BlockSpec(memory_space=pl.ANY)
ROOM = pltpu.CompilerParams(vmem_limit_bytes=56 * 1024 * 1024)


def sine_table(length):
    counts = np.arange(length, dtype=np.int64) + 1
    phase = counts[:, None] * counts[None, :] % (2 * (length + 1))
    table = np.sin(np.pi * phase / (length + 1)).astype(np.float32)
    high = table.astype(ml_dtypes.bfloat16)
    low = (table - high.astype(np.float32)).astype(ml_dtypes.bfloat16)
    return np.stack([high, low])


def laplace_eigen(length):
    counts = np.arange(length, dtype=np.float64) + 1.0
    return 4.0 * np.sin(0.5 * np.pi * counts / (length + 1)) ** 2


def split(value):
    high = value.astype(jnp.bfloat16)
    return high, (value - high.astype(jnp.float32)).astype(jnp.bfloat16)


def dot_pairs(left, right):
    dot = functools.partial(jnp.dot, preferred_element_type=jnp.float32)
    return dot(left[0], right[0]) + (dot(left[0], right[1]) + dot(left[1], right[0]))


def doubled(pair):
    wide = jnp.concatenate(pair, axis=1)
    return jnp.concatenate([wide, wide], axis=0)


def dot_doubled(left, right):
    product = jnp.dot(
        jnp.concatenate(split(left), axis=1), right, preferred_element_type=jnp.float32
    )
    width = product.shape[1] // 2
    return product[:, :width] + product[:, width:]


def power(base, exponent):
    result = None
    while exponent:
        if exponent & 1:
            result = base if result is None else result * base
        exponent >>= 1
        if exponent:
            base = base * base
    return result


def move(source, target, sem):
    copy = pltpu.make_async_copy(source, target, sem)
    copy.start()
    return copy


def loop(count, body):
    lax.fori_loop(0, count, lambda i, _: (body(i), 0)[1], 0)


def unrolled(count, width, body):
    while count % width:
        width //= 2

    def several(i):
        for t in range(width):
            body(i * width + t)

    loop(count // width, several)


def index_kernel(cap, stride, bricks, dest, tag, slot, out):
    half = dest.shape[0] // 2

    def clear(b):
        for end in range(2):
            out[b * stride + cap + end] = 0

    loop(bricks, clear)

    def place(q):
        at = [q, q + half]
        brick = [dest[n] for n in at]
        label = [tag[n] for n in at]
        base = [value * stride for value in brick]
        taken = [out[base[end] + cap + end] for end in range(2)]
        for end in range(2):
            rank = cap - 1 - taken[end] if end else taken[end]
            out[base[end] + cap + end] = taken[end] + 1
            out[base[end] + rank] = label[end]
            slot[at[end]] = brick[end] * (3 * cap) + rank

    unrolled(half, 8, place)


def exchange_kernel(source, bricks, halo, *refs):
    if halo:
        packed, tags, near, courant, out, out_tags, before, after = refs[:8]
        send_sems, recv_sems, rim_send, rim_recv = refs[8:]
    else:
        packed, tags, out, out_tags, send_sems, recv_sems = refs
    grp = lax.axis_index("grp")
    me = lax.axis_index("dev")
    barrier = pltpu.get_barrier_semaphore()

    def greet(i):
        pl.semaphore_signal(
            barrier,
            inc=1,
            device_id=(1 - grp, lax.rem(me + i, bricks)),
            device_id_type=pl.DeviceIdType.MESH,
        )

    loop(bricks, greet)
    neighbours = (lax.rem(me + 1, bricks), lax.rem(me + bricks - 1, bricks))

    @pl.when(grp == source)
    def _():
        if halo:
            for peer in neighbours:
                pl.semaphore_signal(
                    barrier, inc=1, device_id=(grp, peer), device_id_type=pl.DeviceIdType.MESH
                )
        pl.semaphore_wait(barrier, bricks + 2 if halo else bricks)

    @pl.when(grp != source)
    def _():
        pl.semaphore_wait(barrier, bricks)

    def rims():
        if not halo:
            return []
        last = near.shape[1] - 4
        pairs = (
            (near.at[:, pl.ds(last, 4)], before.at[pl.ds(0, 3)]),
            (courant.at[pl.ds(last, 4)], before.at[3]),
            (near.at[:, pl.ds(0, 4)], after.at[pl.ds(0, 3)]),
            (courant.at[pl.ds(0, 4)], after.at[3]),
        )
        return [
            pltpu.make_async_remote_copy(
                src_ref=source_ref,
                dst_ref=target_ref,
                send_sem=rim_send.at[n],
                recv_sem=rim_recv.at[n],
                device_id=(grp, neighbours[n // 2]),
                device_id_type=pl.DeviceIdType.MESH,
            )
            for n, (source_ref, target_ref) in enumerate(pairs)
        ]

    def copies(block, place, peer):
        return [
            pltpu.make_async_remote_copy(
                src_ref=source_ref.at[block],
                dst_ref=target_ref.at[place],
                send_sem=send_sems.at[n, block],
                recv_sem=recv_sems.at[n, place],
                device_id=(1 - grp, peer),
                device_id_type=pl.DeviceIdType.MESH,
            )
            for n, (source_ref, target_ref) in enumerate(((packed, out), (tags, out_tags)))
        ]

    @pl.when(grp == source)
    def _():
        def start(i):
            peer = lax.rem(me + i, bricks)
            for copy in copies(peer, me, peer):
                copy.start()

        def finish(peer):
            for copy in copies(peer, me, peer):
                copy.wait_send()

        loop(bricks, start)
        for copy in rims():
            copy.start()
        for copy in rims():
            copy.wait()
        loop(bricks, finish)

    @pl.when(grp != source)
    def _():
        def finish(peer):
            for copy in copies(peer, peer, peer):
                copy.wait_recv()

        loop(bricks, finish)


def pack_kernel(cap, group, slot, rows, out):
    @pl.when(lax.axis_index("grp") == group)
    def _():
        def place(i):
            first = pl.multiple_of(i * 8, 8)
            slots = [slot[first + t] for t in range(8)]
            for c in range(3):
                tile = rows[c, pl.ds(first, 8), :]
                for t in range(8):
                    out[pl.ds(slots[t] + c * cap, 1), :] = tile[t : t + 1, :]

        loop(rows.shape[1] // 8, place)


def accumulate(cap, stride, bricks, index, arrived, total):
    def from_brick(b):
        base = b * stride

        def add(places):
            rows = [index[base + k] for k in places]
            firsts = [b * (3 * cap) + k for k in places]
            news = [[arrived[pl.ds(n + c * cap, 1), :] for c in range(3)] for n in firsts]
            for row, new in zip(rows, news):
                olds = [total[c, pl.ds(row, 1), :] for c in range(3)]
                for c in range(3):
                    total[c, pl.ds(row, 1), :] = olds[c] + new[c]

        def several(count, place):
            wide = count // 4
            loop(wide, lambda i: add([place(4 * i + t) for t in range(4)]))
            lax.fori_loop(4 * wide, count, lambda k, _: (add([place(k)]), 0)[1], 0)

        several(index[base + cap], lambda k: k)
        several(index[base + cap + 1], lambda k: cap - 1 - k)

    loop(bricks, from_brick)


def forward_kernel(
    cap, stride, bricks, index, arrived, field, decay, table_y, table_z, out, moments, held, sem
):
    planes = field.shape[1] // NY

    @pl.when(lax.axis_index("grp") == 1)
    def _():
        move(field, held, sem).wait()
        accumulate(cap, stride, bricks, index, arrived, held)
        moments[...] = jnp.zeros_like(moments)
        r = decay[0]
        step = 2 - planes % 2

        def plane(i):
            first = i * (step * NY)
            rows = pl.ds(pl.multiple_of(first, NY), step * NY)
            parts = [dot_doubled(held[c, rows, :], table_z[...]) for c in range(3)]
            parts = [part[t * NY : (t + 1) * NY] for t in range(step) for part in parts]
            wide = dot_pairs((table_y[0], table_y[1]), split(jnp.concatenate(parts, axis=1)))
            width = wide.shape[1] // (3 * step)
            for c in range(3):
                total = moments[0, c]
                for t in range(step):
                    n = 3 * t + c
                    now = wide[:, n * width : (n + 1) * width]
                    held[c, pl.ds(pl.multiple_of(first + t * NY, NY), NY), :] = now
                    total = now + r * total
                moments[0, c] = total

        loop(planes // step, plane)
        sent = move(held, out, sem)

        def back(i):
            rows = pl.ds(pl.multiple_of((planes - 1 - i) * NY, NY), NY)
            for c in range(3):
                moments[1, c] = r * (held[c, rows, :] + moments[1, c])

        loop(planes, back)
        sent.wait()


def reduced_kernel(planes, moments, decay, out, got, solved, send_sems, recv_sems, sem):
    bricks = moments.shape[2]
    grp = lax.axis_index("grp")
    me = lax.axis_index("dev")

    @pl.when(grp == 1)
    def _():
        barrier = pltpu.get_barrier_semaphore()

        def greet(i):
            pl.semaphore_signal(
                barrier,
                inc=1,
                device_id=(grp, lax.rem(me + 1 + i, bricks)),
                device_id_type=pl.DeviceIdType.MESH,
            )

        loop(bricks - 1, greet)
        pl.semaphore_wait(barrier, bricks - 1)

        def swap(n, source, target):
            def copy(block, place, peer):
                return pltpu.make_async_remote_copy(
                    src_ref=source.at[:, :, block],
                    dst_ref=target.at[:, :, place],
                    send_sem=send_sems.at[n, block],
                    recv_sem=recv_sems.at[n, place],
                    device_id=(grp, peer),
                    device_id_type=pl.DeviceIdType.MESH,
                )

            def start(i):
                peer = lax.rem(me + 1 + i, bricks)
                copy(peer, me, peer).start()

            def finish(i):
                peer = lax.rem(me + 1 + i, bricks)
                copy(peer, me, peer).wait_send()
                copy(peer, peer, peer).wait_recv()

            loop(bricks - 1, start)
            own = pltpu.make_async_copy(source.at[:, :, me], target.at[:, :, me], sem)
            own.start()
            own.wait()
            loop(bricks - 1, finish)

        swap(0, moments, got)
        r = decay[...]
        r_slab = power(r, planes)
        r_line = power(r, bricks * planes + 1)
        zero = jnp.zeros(got.shape[1:2] + got.shape[3:], jnp.float32)

        def up(d, carry):
            solved[0, :, d] = carry
            return got[0, :, d] + r_slab * carry

        def down(i, carry):
            d = bricks - 1 - i
            solved[1, :, d] = carry
            return got[1, :, d] + r_slab * carry

        right = r * lax.fori_loop(0, bricks, up, zero)
        left = lax.fori_loop(0, bricks, down, zero)
        inverse = 1.0 / (1.0 - r_line * r_line)
        start_value = (right * r_line - left) * inverse
        end_value = (left * r_line - right) * inverse

        def add_up(d, carry):
            solved[0, :, d] += carry
            return r_slab * carry

        def add_down(i, carry):
            d = bricks - 1 - i
            solved[1, :, d] += carry
            return r_slab * carry

        lax.fori_loop(0, bricks, add_up, start_value)
        lax.fori_loop(0, bricks, add_down, r * end_value)
        swap(1, solved, out)


def backward_kernel(
    row, spectral, edges, decay, table_y, table_z, remesh_t, _fields, fields, interp, held, pot, run, sem
):
    planes = spectral.shape[1] // NY

    @pl.when(lax.axis_index("grp") == 1)
    def _():
        move(spectral, held, sem).wait()
        r = decay[0]
        gain = decay[1]
        run[...] = edges[...]

        def rows_of(i):
            return pl.ds(pl.multiple_of(i * NY, NY), NY)

        def potential(places, modes):
            wide = dot_pairs((table_y[0], table_y[1]), split(jnp.concatenate(modes, axis=1)))
            width = wide.shape[1] // len(modes)
            parts = [wide[:, n * width : (n + 1) * width] for n in range(len(modes))]
            for c in range(3):
                tall = dot_doubled(jnp.concatenate(parts[c::3], axis=0), table_z[...])
                for t, place in enumerate(places):
                    pot[c, rows_of(place), :] = tall[t * NY : (t + 1) * NY]

        def back(i):
            at = planes - 1 - i
            for c in range(3):
                q = run[1, c]
                pot[c, rows_of(at + 1), :] = q
                run[1, c] = r * (held[c, rows_of(at), :] + q)

        loop(planes, back)
        step = 2 - planes % 2

        def ahead(i):
            modes = []
            for t in range(step):
                at = i * step + t
                for c in range(3):
                    p = held[c, rows_of(at), :] + r * run[0, c]
                    run[0, c] = p
                    modes.append(gain * (p + pot[c, rows_of(at + 1), :]))
            potential([i * step + t + 1 for t in range(step)], modes)

        loop(planes // step, ahead)
        below = [gain * (edges[0, c] + run[1, c]) for c in range(3)]
        above = [gain * (r * run[0, c] + edges[1, c] / r) for c in range(3)]
        potential([0, planes + 1], below + above)

        depth = pot.shape[2]
        y_at = lax.broadcasted_iota(jnp.int32, (NY, depth), 0)
        z_at = lax.broadcasted_iota(jnp.int32, (NY, depth), 1)

        def d_y(f):
            upper = jnp.where(y_at == NY - 1, 0.0, pltpu.roll(f, NY - 1, 0))
            return upper - jnp.where(y_at == 0, 0.0, pltpu.roll(f, 1, 0))

        def d_z(f):
            upper = jnp.where(z_at == depth - 1, 0.0, pltpu.roll(f, depth - 1, 1))
            return upper - jnp.where(z_at == 0, 0.0, pltpu.roll(f, 1, 1))

        def curl(i):
            here = rows_of(i + 1)
            f = [pot[c, here, :] for c in range(3)]
            slope_y = pot[1, rows_of(i + 2), :] - pot[1, rows_of(i), :]
            slope_z = pot[2, rows_of(i + 2), :] - pot[2, rows_of(i), :]
            held[0, rows_of(i), :] = 0.5 * (d_y(f[2]) - d_z(f[1]))
            held[1, rows_of(i), :] = 0.5 * (d_z(f[0]) - slope_z)
            held[2, rows_of(i), :] = 0.5 * (slope_y - d_y(f[0]))

        loop(planes, curl)
        sent = move(held, fields, sem)

        def pick(i):
            first = pl.multiple_of(i * 8, 8)
            places = [row[first + t] for t in range(8)]
            for c in range(3):
                for t in range(8):
                    interp[c, pl.ds(first + t, 1), :] = held[c, pl.ds(places[t], 1), :]

        loop(interp.shape[1] // 8, pick)
        weights = doubled(split(remesh_t[...]))
        count = min(256, interp.shape[1])

        def project(i):
            rows = pl.ds(pl.multiple_of(i * count, count), count)
            for c in range(3):
                interp[c, rows, :] = dot_doubled(interp[c, rows, :], weights)

        loop(interp.shape[1] // count, project)
        sent.wait()


def advance_kernel(near, courant, before, after, out, ext, first, sems):
    rows_j = near.shape[1]

    @pl.when(lax.axis_index("grp") == 0)
    def _():
        copies = [
            move(near, ext.at[pl.ds(0, 3), pl.ds(4, rows_j)], sems.at[0]),
            move(courant, ext.at[3, pl.ds(4, rows_j)], sems.at[1]),
            move(before, ext.at[:, pl.ds(0, 4)], sems.at[2]),
            move(after, ext.at[:, pl.ds(rows_j + 4, 4)], sems.at[3]),
        ]
        for copy in copies:
            copy.wait()
        i_at = lax.broadcasted_iota(jnp.int32, near.shape[2:], 0)

        def stepped(f, speed):
            transport = (8.0 * (f[3] - f[1]) - (f[4] - f[0])) * (1.0 / 12.0)
            upper = jnp.where(i_at == NI - 1, 0.0, pltpu.roll(f[2], NI - 1, 0))
            lower = jnp.where(i_at == 0, 0.0, pltpu.roll(f[2], 1, 0))
            return f[2] - speed * transport + viscosity * (upper - 2.0 * f[2] + lower)

        def one(j):
            speed = ext[3, j + 2]
            for c in range(3):
                first[c, j] = stepped([ext[c, j + t] for t in range(5)], speed)

        loop(rows_j + 4, one)

        def two(j):
            speed = ext[3, j + 4]
            for c in range(3):
                ext[c, j] = stepped([first[c, j + t] for t in range(5)], speed)

        loop(rows_j, two)
        move(ext.at[pl.ds(0, 3), pl.ds(0, rows_j)], out, sems.at[0]).wait()


def finish_kernel(cap, stride, bricks, index, arrived, layer, _fields, fields, boundary, rim, sem):
    @pl.when(lax.axis_index("grp") == 0)
    def _():
        fetched = move(fields.at[:, :, pl.ds(NI - 8, 8), :], rim, sem)
        boundary[...] = jnp.zeros_like(boundary)
        accumulate(cap, stride, bricks, index, arrived, boundary)
        fetched.wait()
        for c in range(3):
            a, b = (c + 1) % 3, (c + 2) % 3
            turned = coupling * (boundary[a] * layer[b] - boundary[b] * layer[a])
            rim[c, :, 7, :] += turned
        move(rim, fields.at[:, :, pl.ds(NI - 8, 8), :], sem).wait()


def on_device(state, courant, remesh, shell_dest, shell_row, return_dest, return_row, return_block):
    bricks = lax.axis_size("dev")
    cell_count = state.shape[2]
    span_cells, lattice_z = remesh.shape
    rows_j = cell_count // (NI * span_cells)
    shell_depth = NI // 4
    shell_blocks = shell_depth * rows_j
    cap = 2 * shell_blocks // bricks
    stride = -(-(cap + 2) // 128) * 128
    planes = NX // bricks
    slab_rows = planes * NY
    f32 = functools.partial(jax.ShapeDtypeStruct, dtype=jnp.float32)
    i32 = functools.partial(jax.ShapeDtypeStruct, dtype=jnp.int32)
    field = state[0].reshape(3, slab_rows, lattice_z)
    near = field.reshape(3, rows_j, NI, span_cells)

    blocks = near[:, :, NI - shell_depth :, :].reshape(3, shell_blocks, span_cells)
    remeshed = jnp.einsum("cqk,kz->cqz", blocks, remesh, precision=lax.Precision.HIGH)

    courant_near = courant.reshape(rows_j, NI, span_cells)
    on_near = lax.axis_index("grp") == 0
    slots, tags = pl.pallas_call(
        functools.partial(index_kernel, cap, stride, bricks),
        out_shape=(i32((shell_blocks,)), i32((bricks * stride,))),
        in_specs=[SMEM] * 2,
        out_specs=(SMEM,) * 2,
    )(
        jnp.where(on_near, shell_dest[:, 0], return_dest[:, 0]),
        jnp.where(on_near, shell_row, return_block),
    )
    tags = tags.reshape(bricks, stride // 128, 128)

    def pack(rows, slots, group):
        return pl.pallas_call(
            functools.partial(pack_kernel, cap, group),
            out_shape=f32((bricks * 3 * cap, lattice_z)),
            in_specs=[SMEM, VMEM],
            out_specs=VMEM,
            compiler_params=ROOM,
        )(slots, rows).reshape(bricks, 3 * cap, lattice_z)

    def exchange(packed, group, *edge):
        rim = f32((4, 4, NI, span_cells))
        extra = 2 if edge else 0
        arrived, index, *rims = pl.pallas_call(
            functools.partial(exchange_kernel, group, bricks, bool(edge)),
            out_shape=(
                f32((bricks, 3 * cap, lattice_z)),
                i32((bricks, stride // 128, 128)),
                *[rim] * extra,
            ),
            in_specs=[HBM] * (2 + extra),
            out_specs=(HBM,) * (2 + extra),
            scratch_shapes=[pltpu.SemaphoreType.DMA((2, bricks))] * 2
            + [pltpu.SemaphoreType.DMA((4,))] * extra,
            compiler_params=pltpu.CompilerParams(collective_id=group, has_side_effects=True),
        )(packed, tags, *edge)
        return arrived.reshape(bricks * 3 * cap, lattice_z), index.reshape(-1), *rims

    arrived, index, before, after = exchange(pack(remeshed, slots, 0), 0, near, courant_near)

    table_y = sine_table(NY)
    table_z = np.tile(np.concatenate(list(sine_table(lattice_z)), axis=1), (2, 1))
    total = laplace_eigen(NY)[:, None] + laplace_eigen(lattice_z)[None, :]
    root = np.sqrt(total * (total + 4.0))
    decay = 2.0 / (2.0 + total + root)
    scale = 4.0 / ((NY + 1) * (lattice_z + 1))
    factors = jnp.asarray(np.stack([decay, scale / root]), jnp.float32)

    spectral, moments = pl.pallas_call(
        functools.partial(forward_kernel, cap, stride, bricks),
        out_shape=(f32((3, slab_rows, lattice_z)), f32((2, 3, NY, lattice_z))),
        in_specs=[SMEM, VMEM, HBM, VMEM, VMEM, VMEM],
        out_specs=(HBM, VMEM),
        scratch_shapes=[pltpu.VMEM((3, slab_rows, lattice_z), jnp.float32), pltpu.SemaphoreType.DMA],
        compiler_params=ROOM,
    )(index, arrived, field, factors, table_y, table_z)

    advanced = pl.pallas_call(
        advance_kernel,
        out_shape=f32((3, rows_j, NI, span_cells)),
        in_specs=[HBM] * 4,
        out_specs=HBM,
        scratch_shapes=[
            pltpu.VMEM((4, rows_j + 8, NI, span_cells), jnp.float32),
            pltpu.VMEM((3, rows_j + 4, NI, span_cells), jnp.float32),
            pltpu.SemaphoreType.DMA((4,)),
        ],
        compiler_params=ROOM,
    )(near, courant_near, before, after)

    lines = NY // bricks
    mine = lax.dynamic_slice_in_dim(factors[0], lax.axis_index("dev") * lines, lines)
    shared = (2, 3, bricks, lines, lattice_z)
    edges = pl.pallas_call(
        functools.partial(reduced_kernel, planes),
        out_shape=f32(shared),
        in_specs=[VMEM, VMEM],
        out_specs=VMEM,
        scratch_shapes=[pltpu.VMEM(shared, jnp.float32)] * 2
        + [pltpu.SemaphoreType.DMA((2, bricks))] * 2
        + [pltpu.SemaphoreType.DMA],
        compiler_params=pltpu.CompilerParams(
            collective_id=2, has_side_effects=True, vmem_limit_bytes=32 * 1024 * 1024
        ),
    )(moments.reshape(shared), mine).reshape(2, 3, NY, lattice_z)

    fields, interp = pl.pallas_call(
        backward_kernel,
        out_shape=(f32((3, slab_rows, lattice_z)), f32((3, shell_blocks, span_cells))),
        in_specs=[SMEM, HBM, VMEM, VMEM, VMEM, VMEM, VMEM, HBM],
        out_specs=(HBM, VMEM),
        scratch_shapes=[
            pltpu.VMEM((3, slab_rows, lattice_z), jnp.float32),
            pltpu.VMEM((3, slab_rows + 2 * NY, lattice_z), jnp.float32),
            pltpu.VMEM((2, 3, NY, lattice_z), jnp.float32),
            pltpu.SemaphoreType.DMA,
        ],
        input_output_aliases={7: 0},
        compiler_params=ROOM,
    )(
        return_row,
        spectral,
        edges,
        factors,
        table_y,
        table_z,
        remesh.T,
        advanced.reshape(3, slab_rows, lattice_z),
    )

    returned, index_back = exchange(pack(interp, slots, 1), 1)
    fields = pl.pallas_call(
        functools.partial(finish_kernel, cap, stride, bricks),
        out_shape=f32((3, rows_j, NI, span_cells)),
        in_specs=[SMEM, VMEM, VMEM, HBM],
        out_specs=HBM,
        scratch_shapes=[
            pltpu.VMEM((3, rows_j, span_cells), jnp.float32),
            pltpu.VMEM((3, rows_j, 8, span_cells), jnp.float32),
            pltpu.SemaphoreType.DMA,
        ],
        input_output_aliases={3: 0},
        compiler_params=ROOM,
    )(index_back, returned, near[:, :, NI - 1, :], fields.reshape(3, rows_j, NI, span_cells))
    return fields.reshape(1, 3, cell_count)


def solution(mesh):
    placed = (
        P("grp", None, "dev"),
        P("dev"),
        P(),
        P("dev", None),
        P("dev"),
        P("dev", None),
        P("dev"),
        P("dev"),
    )
    return jax.shard_map(
        on_device, mesh=mesh, in_specs=placed, out_specs=P("grp", None, "dev"), check_vma=False
    )
```

```python
import functools

import jax
import jax.numpy as jnp
import ml_dtypes
import numpy as np
from jax import lax
from jax.experimental import pallas as pl
from jax.experimental.pallas import tpu as pltpu
from jax.sharding import PartitionSpec as P

NX = 512
NY = 256
NI = 64

viscosity = 0.2
coupling = 1.0

VMEM = pl.BlockSpec(memory_space=pltpu.VMEM)
SMEM = pl.BlockSpec(memory_space=pltpu.SMEM)
HBM = pl.BlockSpec(memory_space=pl.ANY)
ROOM = pltpu.CompilerParams(vmem_limit_bytes=56 * 1024 * 1024)


def sine_table(length):
    counts = np.arange(length, dtype=np.int64) + 1
    phase = counts[:, None] * counts[None, :] % (2 * (length + 1))
    table = np.sin(np.pi * phase / (length + 1)).astype(np.float32)
    high = table.astype(ml_dtypes.bfloat16)
    low = (table - high.astype(np.float32)).astype(ml_dtypes.bfloat16)
    return np.stack([high, low])


def laplace_eigen(length):
    counts = np.arange(length, dtype=np.float64) + 1.0
    return 4.0 * np.sin(0.5 * np.pi * counts / (length + 1)) ** 2


def split(value):
    high = value.astype(jnp.bfloat16)
    return high, (value - high.astype(jnp.float32)).astype(jnp.bfloat16)


def dot_pairs(left, right):
    dot = functools.partial(jnp.dot, preferred_element_type=jnp.float32)
    return dot(left[0], right[0]) + (dot(left[0], right[1]) + dot(left[1], right[0]))


def doubled(pair):
    wide = jnp.concatenate(pair, axis=1)
    return jnp.concatenate([wide, wide], axis=0)


def dot_doubled(left, right):
    product = jnp.dot(
        jnp.concatenate(split(left), axis=1), right, preferred_element_type=jnp.float32
    )
    width = product.shape[1] // 2
    return product[:, :width] + product[:, width:]


def power(base, exponent):
    result = None
    while exponent:
        if exponent & 1:
            result = base if result is None else result * base
        exponent >>= 1
        if exponent:
            base = base * base
    return result


def move(source, target, sem):
    copy = pltpu.make_async_copy(source, target, sem)
    copy.start()
    return copy


def loop(count, body):
    lax.fori_loop(0, count, lambda i, _: (body(i), 0)[1], 0)


def unrolled(count, width, body):
    while count % width:
        width //= 2

    def several(i):
        for t in range(width):
            body(i * width + t)

    loop(count // width, several)


def index_kernel(cap, stride, bricks, dest_a, tag_a, dest_b, tag_b, slot, out):
    half = dest_a.shape[0] // 2

    def clear(b):
        for end in range(2):
            out[b * stride + cap + end] = 0

    loop(bricks, clear)

    def place(dest, tag, q):
        at = [q, q + half]
        brick = [dest[n] for n in at]
        label = [tag[n] for n in at]
        base = [value * stride for value in brick]
        taken = [out[base[end] + cap + end] for end in range(2)]
        for end in range(2):
            rank = cap - 1 - taken[end] if end else taken[end]
            out[base[end] + cap + end] = taken[end] + 1
            out[base[end] + rank] = label[end]
            slot[at[end]] = brick[end] * (3 * cap) + rank

    for group, sides in enumerate(((dest_a, tag_a), (dest_b, tag_b))):

        @pl.when(lax.axis_index("grp") == group)
        def _(sides=sides):
            unrolled(half, 8, functools.partial(place, *sides))


def exchange_kernel(source, bricks, halo, *refs):
    if halo:
        packed, tags, near, courant, out, out_tags, before, after = refs[:8]
        send_sems, recv_sems, rim_send, rim_recv = refs[8:]
    else:
        packed, tags, out, out_tags, send_sems, recv_sems = refs
    grp = lax.axis_index("grp")
    me = lax.axis_index("dev")
    barrier = pltpu.get_barrier_semaphore()

    def greet(i):
        pl.semaphore_signal(
            barrier,
            inc=1,
            device_id=(1 - grp, lax.rem(me + i, bricks)),
            device_id_type=pl.DeviceIdType.MESH,
        )

    loop(bricks, greet)
    neighbours = (lax.rem(me + 1, bricks), lax.rem(me + bricks - 1, bricks))

    @pl.when(grp == source)
    def _():
        if halo:
            for peer in neighbours:
                pl.semaphore_signal(
                    barrier, inc=1, device_id=(grp, peer), device_id_type=pl.DeviceIdType.MESH
                )
        pl.semaphore_wait(barrier, bricks + 2 if halo else bricks)

    @pl.when(grp != source)
    def _():
        pl.semaphore_wait(barrier, bricks)

    def rims():
        if not halo:
            return []
        last = near.shape[1] - 4
        pairs = (
            (near.at[:, pl.ds(last, 4)], before.at[pl.ds(0, 3)]),
            (courant.at[pl.ds(last, 4)], before.at[3]),
            (near.at[:, pl.ds(0, 4)], after.at[pl.ds(0, 3)]),
            (courant.at[pl.ds(0, 4)], after.at[3]),
        )
        return [
            pltpu.make_async_remote_copy(
                src_ref=source_ref,
                dst_ref=target_ref,
                send_sem=rim_send.at[n],
                recv_sem=rim_recv.at[n],
                device_id=(grp, neighbours[n // 2]),
                device_id_type=pl.DeviceIdType.MESH,
            )
            for n, (source_ref, target_ref) in enumerate(pairs)
        ]

    def copies(block, place, peer):
        return [
            pltpu.make_async_remote_copy(
                src_ref=source_ref.at[block],
                dst_ref=target_ref.at[place],
                send_sem=send_sems.at[n, block],
                recv_sem=recv_sems.at[n, place],
                device_id=(1 - grp, peer),
                device_id_type=pl.DeviceIdType.MESH,
            )
            for n, (source_ref, target_ref) in enumerate(((packed, out), (tags, out_tags)))
        ]

    @pl.when(grp == source)
    def _():
        def start(i):
            peer = lax.rem(me + i, bricks)
            for copy in copies(peer, me, peer):
                copy.start()

        def finish(peer):
            for copy in copies(peer, me, peer):
                copy.wait_send()

        loop(bricks, start)
        for copy in rims():
            copy.start()
        for copy in rims():
            copy.wait()
        loop(bricks, finish)

    @pl.when(grp != source)
    def _():
        def finish(peer):
            for copy in copies(peer, peer, peer):
                copy.wait_recv()

        loop(bricks, finish)


def pack_kernel(cap, slot, near, remesh, out, shell, sem):
    rows_j = near.shape[1]
    depth = shell.shape[2]

    @pl.when(lax.axis_index("grp") == 0)
    def _():
        move(near.at[:, :, pl.ds(NI - depth, depth), :], shell, sem).wait()
        weights = doubled(split(remesh[...]))
        count = min(16, rows_j)

        def project(i):
            for c in range(3):
                block = shell[c, pl.ds(i * count, count)]
                block = block.reshape(count * depth, block.shape[2])
                block = dot_doubled(block, weights)
                shell[c, pl.ds(i * count, count)] = block.reshape(count, depth, block.shape[1])

        loop(rows_j // count, project)

        def place(j):
            for half in range(depth // 8):
                slots = [slot[j * depth + half * 8 + t] for t in range(8)]
                for c in range(3):
                    tile = shell[c, j, half * 8 : half * 8 + 8, :]
                    for t in range(8):
                        out[pl.ds(slots[t] + c * cap, 1), :] = tile[t : t + 1, :]

        loop(rows_j, place)


def accumulate(cap, stride, bricks, index, arrived, total):
    def from_brick(b):
        base = b * stride

        def add(places):
            rows = [index[base + k] for k in places]
            firsts = [b * (3 * cap) + k for k in places]
            news = [[arrived[pl.ds(n + c * cap, 1), :] for c in range(3)] for n in firsts]
            for row, new in zip(rows, news):
                olds = [total[c, pl.ds(row, 1), :] for c in range(3)]
                for c in range(3):
                    total[c, pl.ds(row, 1), :] = olds[c] + new[c]

        def several(count, place):
            wide = count // 4
            loop(wide, lambda i: add([place(4 * i + t) for t in range(4)]))
            lax.fori_loop(4 * wide, count, lambda k, _: (add([place(k)]), 0)[1], 0)

        several(index[base + cap], lambda k: k)
        several(index[base + cap + 1], lambda k: cap - 1 - k)

    loop(bricks, from_brick)


def forward_kernel(
    cap, stride, bricks, index, arrived, field, decay, table_y, table_z, out, moments, held, sem
):
    planes = field.shape[1] // NY

    @pl.when(lax.axis_index("grp") == 1)
    def _():
        move(field, held, sem).wait()
        accumulate(cap, stride, bricks, index, arrived, held)
        moments[...] = jnp.zeros_like(moments)
        r = decay[0]
        step = 2 - planes % 2

        def plane(i):
            first = i * (step * NY)
            rows = pl.ds(pl.multiple_of(first, NY), step * NY)
            parts = [dot_doubled(held[c, rows, :], table_z[...]) for c in range(3)]
            parts = [part[t * NY : (t + 1) * NY] for t in range(step) for part in parts]
            wide = dot_pairs((table_y[0], table_y[1]), split(jnp.concatenate(parts, axis=1)))
            width = wide.shape[1] // (3 * step)
            for c in range(3):
                total = moments[0, c]
                for t in range(step):
                    n = 3 * t + c
                    now = wide[:, n * width : (n + 1) * width]
                    held[c, pl.ds(pl.multiple_of(first + t * NY, NY), NY), :] = now
                    total = now + r * total
                moments[0, c] = total

        loop(planes // step, plane)
        sent = move(held, out, sem)

        def back(i):
            rows = pl.ds(pl.multiple_of((planes - 1 - i) * NY, NY), NY)
            for c in range(3):
                moments[1, c] = r * (held[c, rows, :] + moments[1, c])

        loop(planes, back)
        sent.wait()


def reduced_kernel(planes, moments, decay, out, got, solved, send_sems, recv_sems, sem):
    bricks = moments.shape[2]
    grp = lax.axis_index("grp")
    me = lax.axis_index("dev")

    @pl.when(grp == 1)
    def _():
        barrier = pltpu.get_barrier_semaphore()

        def greet(i):
            pl.semaphore_signal(
                barrier,
                inc=1,
                device_id=(grp, lax.rem(me + 1 + i, bricks)),
                device_id_type=pl.DeviceIdType.MESH,
            )

        loop(bricks - 1, greet)
        pl.semaphore_wait(barrier, bricks - 1)

        def swap(n, source, target):
            def copy(block, place, peer):
                return pltpu.make_async_remote_copy(
                    src_ref=source.at[:, :, block],
                    dst_ref=target.at[:, :, place],
                    send_sem=send_sems.at[n, block],
                    recv_sem=recv_sems.at[n, place],
                    device_id=(grp, peer),
                    device_id_type=pl.DeviceIdType.MESH,
                )

            def start(i):
                peer = lax.rem(me + 1 + i, bricks)
                copy(peer, me, peer).start()

            def finish(i):
                peer = lax.rem(me + 1 + i, bricks)
                copy(peer, me, peer).wait_send()
                copy(peer, peer, peer).wait_recv()

            loop(bricks - 1, start)
            own = pltpu.make_async_copy(source.at[:, :, me], target.at[:, :, me], sem)
            own.start()
            own.wait()
            loop(bricks - 1, finish)

        swap(0, moments, got)
        r = decay[...]
        r_slab = power(r, planes)
        r_line = power(r, bricks * planes + 1)
        zero = jnp.zeros(got.shape[1:2] + got.shape[3:], jnp.float32)

        def up(d, carry):
            solved[0, :, d] = carry
            return got[0, :, d] + r_slab * carry

        def down(i, carry):
            d = bricks - 1 - i
            solved[1, :, d] = carry
            return got[1, :, d] + r_slab * carry

        right = r * lax.fori_loop(0, bricks, up, zero)
        left = lax.fori_loop(0, bricks, down, zero)
        inverse = 1.0 / (1.0 - r_line * r_line)
        start_value = (right * r_line - left) * inverse
        end_value = (left * r_line - right) * inverse

        def add_up(d, carry):
            solved[0, :, d] += carry
            return r_slab * carry

        def add_down(i, carry):
            d = bricks - 1 - i
            solved[1, :, d] += carry
            return r_slab * carry

        lax.fori_loop(0, bricks, add_up, start_value)
        lax.fori_loop(0, bricks, add_down, r * end_value)
        swap(1, solved, out)


def backward_kernel(
    cap,
    row,
    slot,
    spectral,
    edges,
    decay,
    table_y,
    table_z,
    remesh_t,
    _fields,
    fields,
    packed,
    held,
    pot,
    run,
    sem,
):
    planes = spectral.shape[1] // NY

    @pl.when(lax.axis_index("grp") == 1)
    def _():
        move(spectral, held, sem).wait()
        r = decay[0]
        gain = decay[1]
        run[...] = edges[...]

        def rows_of(i):
            return pl.ds(pl.multiple_of(i * NY, NY), NY)

        def potential(places, modes):
            wide = dot_pairs((table_y[0], table_y[1]), split(jnp.concatenate(modes, axis=1)))
            width = wide.shape[1] // len(modes)
            parts = [wide[:, n * width : (n + 1) * width] for n in range(len(modes))]
            for c in range(3):
                tall = dot_doubled(jnp.concatenate(parts[c::3], axis=0), table_z[...])
                for t, place in enumerate(places):
                    pot[c, rows_of(place), :] = tall[t * NY : (t + 1) * NY]

        def back(i):
            at = planes - 1 - i
            for c in range(3):
                q = run[1, c]
                pot[c, rows_of(at + 1), :] = q
                run[1, c] = r * (held[c, rows_of(at), :] + q)

        loop(planes, back)
        step = 2 - planes % 2

        def ahead(i):
            modes = []
            for t in range(step):
                at = i * step + t
                for c in range(3):
                    p = held[c, rows_of(at), :] + r * run[0, c]
                    run[0, c] = p
                    modes.append(gain * (p + pot[c, rows_of(at + 1), :]))
            potential([i * step + t + 1 for t in range(step)], modes)

        loop(planes // step, ahead)
        below = [gain * (edges[0, c] + run[1, c]) for c in range(3)]
        above = [gain * (r * run[0, c] + edges[1, c] / r) for c in range(3)]
        potential([0, planes + 1], below + above)

        depth = pot.shape[2]
        y_at = lax.broadcasted_iota(jnp.int32, (NY, depth), 0)
        z_at = lax.broadcasted_iota(jnp.int32, (NY, depth), 1)

        def d_y(f):
            upper = jnp.where(y_at == NY - 1, 0.0, pltpu.roll(f, NY - 1, 0))
            return upper - jnp.where(y_at == 0, 0.0, pltpu.roll(f, 1, 0))

        def d_z(f):
            upper = jnp.where(z_at == depth - 1, 0.0, pltpu.roll(f, depth - 1, 1))
            return upper - jnp.where(z_at == 0, 0.0, pltpu.roll(f, 1, 1))

        def curl(i):
            here = rows_of(i + 1)
            f = [pot[c, here, :] for c in range(3)]
            slope_y = pot[1, rows_of(i + 2), :] - pot[1, rows_of(i), :]
            slope_z = pot[2, rows_of(i + 2), :] - pot[2, rows_of(i), :]
            held[0, rows_of(i), :] = 0.5 * (d_y(f[2]) - d_z(f[1]))
            held[1, rows_of(i), :] = 0.5 * (d_z(f[0]) - slope_z)
            held[2, rows_of(i), :] = 0.5 * (slope_y - d_y(f[0]))

        loop(planes, curl)
        sent = move(held, fields, sem)

        def pick(i):
            first = pl.multiple_of(i * 8, 8)
            places = [row[first + t] for t in range(8)]
            slots = [slot[first + t] for t in range(8)]
            for t in range(8):
                picked = [held[c, pl.ds(places[t], 1), :] for c in range(3)]
                for c in range(3):
                    packed[pl.ds(slots[t] + c * cap, 1), :] = picked[c]

        loop(row.shape[0] // 8, pick)
        weights = doubled(split(remesh_t[...]))
        count = 512 if packed.shape[0] % 512 == 0 else packed.shape[0]

        def project(i):
            rows = pl.ds(pl.multiple_of(i * count, count), count)
            packed[rows, :] = dot_doubled(packed[rows, :], weights)

        loop(packed.shape[0] // count, project)
        sent.wait()


def advance_kernel(near, courant, before, after, out, ext, first, sems):
    rows_j = near.shape[1]

    @pl.when(lax.axis_index("grp") == 0)
    def _():
        copies = [
            move(near, ext.at[pl.ds(0, 3), pl.ds(4, rows_j)], sems.at[0]),
            move(courant, ext.at[3, pl.ds(4, rows_j)], sems.at[1]),
            move(before, ext.at[:, pl.ds(0, 4)], sems.at[2]),
            move(after, ext.at[:, pl.ds(rows_j + 4, 4)], sems.at[3]),
        ]
        for copy in copies:
            copy.wait()
        i_at = lax.broadcasted_iota(jnp.int32, near.shape[2:], 0)

        def stepped(f, speed):
            transport = (8.0 * (f[3] - f[1]) - (f[4] - f[0])) * (1.0 / 12.0)
            upper = jnp.where(i_at == NI - 1, 0.0, pltpu.roll(f[2], NI - 1, 0))
            lower = jnp.where(i_at == 0, 0.0, pltpu.roll(f[2], 1, 0))
            return f[2] - speed * transport + viscosity * (upper - 2.0 * f[2] + lower)

        def one(j):
            speed = ext[3, j + 2]
            for c in range(3):
                first[c, j] = stepped([ext[c, j + t] for t in range(5)], speed)

        loop(rows_j + 4, one)

        def two(j):
            speed = ext[3, j + 4]
            for c in range(3):
                ext[c, j] = stepped([first[c, j + t] for t in range(5)], speed)

        loop(rows_j, two)
        move(ext.at[pl.ds(0, 3), pl.ds(0, rows_j)], out, sems.at[0]).wait()


def finish_kernel(cap, stride, bricks, index, arrived, near, _fields, fields, boundary, rim, layer, sems):
    @pl.when(lax.axis_index("grp") == 0)
    def _():
        top = pl.ds(NI - 8, 8)
        fetched = move(fields.at[:, :, top, :], rim, sems.at[0])
        known = move(near.at[:, :, top, :], layer, sems.at[1])
        boundary[...] = jnp.zeros_like(boundary)
        accumulate(cap, stride, bricks, index, arrived, boundary)
        fetched.wait()
        known.wait()
        for c in range(3):
            a, b = (c + 1) % 3, (c + 2) % 3
            turned = coupling * (
                boundary[a] * layer[b, :, 7, :] - boundary[b] * layer[a, :, 7, :]
            )
            rim[c, :, 7, :] += turned
        move(rim, fields.at[:, :, top, :], sems.at[0]).wait()


def on_device(state, courant, remesh, shell_dest, shell_row, return_dest, return_row, return_block):
    bricks = lax.axis_size("dev")
    cell_count = state.shape[2]
    span_cells, lattice_z = remesh.shape
    rows_j = cell_count // (NI * span_cells)
    shell_depth = NI // 4
    shell_blocks = shell_depth * rows_j
    cap = 2 * shell_blocks // bricks
    stride = -(-(cap + 2) // 128) * 128
    planes = NX // bricks
    slab_rows = planes * NY
    f32 = functools.partial(jax.ShapeDtypeStruct, dtype=jnp.float32)
    i32 = functools.partial(jax.ShapeDtypeStruct, dtype=jnp.int32)
    field = state[0].reshape(3, slab_rows, lattice_z)
    near = field.reshape(3, rows_j, NI, span_cells)

    courant_near = courant.reshape(rows_j, NI, span_cells)
    slots, tags = pl.pallas_call(
        functools.partial(index_kernel, cap, stride, bricks),
        out_shape=(i32((shell_blocks,)), i32((bricks * stride,))),
        in_specs=[SMEM] * 4,
        out_specs=(SMEM,) * 2,
    )(shell_dest[:, 0], shell_row, return_dest[:, 0], return_block)
    tags = tags.reshape(bricks, stride // 128, 128)

    packed_shell = pl.pallas_call(
        functools.partial(pack_kernel, cap),
        out_shape=f32((bricks * 3 * cap, lattice_z)),
        in_specs=[SMEM, HBM, VMEM],
        out_specs=VMEM,
        scratch_shapes=[
            pltpu.VMEM((3, rows_j, shell_depth, span_cells), jnp.float32),
            pltpu.SemaphoreType.DMA,
        ],
        compiler_params=ROOM,
    )(slots, near, remesh)

    def exchange(packed, group, *edge):
        rim = f32((4, 4, NI, span_cells))
        extra = 2 if edge else 0
        arrived, index, *rims = pl.pallas_call(
            functools.partial(exchange_kernel, group, bricks, bool(edge)),
            out_shape=(
                f32((bricks, 3 * cap, lattice_z)),
                i32((bricks, stride // 128, 128)),
                *[rim] * extra,
            ),
            in_specs=[HBM] * (2 + extra),
            out_specs=(HBM,) * (2 + extra),
            scratch_shapes=[pltpu.SemaphoreType.DMA((2, bricks))] * 2
            + [pltpu.SemaphoreType.DMA((4,))] * extra,
            compiler_params=pltpu.CompilerParams(collective_id=group, has_side_effects=True),
        )(packed.reshape(bricks, 3 * cap, lattice_z), tags, *edge)
        return arrived.reshape(bricks * 3 * cap, lattice_z), index.reshape(-1), *rims

    arrived, index, before, after = exchange(packed_shell, 0, near, courant_near)

    table_y = sine_table(NY)
    table_z = np.tile(np.concatenate(list(sine_table(lattice_z)), axis=1), (2, 1))
    total = laplace_eigen(NY)[:, None] + laplace_eigen(lattice_z)[None, :]
    root = np.sqrt(total * (total + 4.0))
    decay = 2.0 / (2.0 + total + root)
    scale = 4.0 / ((NY + 1) * (lattice_z + 1))
    factors = jnp.asarray(np.stack([decay, scale / root]), jnp.float32)

    spectral, moments = pl.pallas_call(
        functools.partial(forward_kernel, cap, stride, bricks),
        out_shape=(f32((3, slab_rows, lattice_z)), f32((2, 3, NY, lattice_z))),
        in_specs=[SMEM, VMEM, HBM, VMEM, VMEM, VMEM],
        out_specs=(HBM, VMEM),
        scratch_shapes=[pltpu.VMEM((3, slab_rows, lattice_z), jnp.float32), pltpu.SemaphoreType.DMA],
        compiler_params=ROOM,
    )(index, arrived, field, factors, table_y, table_z)

    advanced = pl.pallas_call(
        advance_kernel,
        out_shape=f32((3, rows_j, NI, span_cells)),
        in_specs=[HBM] * 4,
        out_specs=HBM,
        scratch_shapes=[
            pltpu.VMEM((4, rows_j + 8, NI, span_cells), jnp.float32),
            pltpu.VMEM((3, rows_j + 4, NI, span_cells), jnp.float32),
            pltpu.SemaphoreType.DMA((4,)),
        ],
        compiler_params=ROOM,
    )(near, courant_near, before, after)

    lines = NY // bricks
    mine = lax.dynamic_slice_in_dim(factors[0], lax.axis_index("dev") * lines, lines)
    shared = (2, 3, bricks, lines, lattice_z)
    edges = pl.pallas_call(
        functools.partial(reduced_kernel, planes),
        out_shape=f32(shared),
        in_specs=[VMEM, VMEM],
        out_specs=VMEM,
        scratch_shapes=[pltpu.VMEM(shared, jnp.float32)] * 2
        + [pltpu.SemaphoreType.DMA((2, bricks))] * 2
        + [pltpu.SemaphoreType.DMA],
        compiler_params=pltpu.CompilerParams(
            collective_id=2, has_side_effects=True, vmem_limit_bytes=32 * 1024 * 1024
        ),
    )(moments.reshape(shared), mine).reshape(2, 3, NY, lattice_z)

    fields, packed_back = pl.pallas_call(
        functools.partial(backward_kernel, cap),
        out_shape=(f32((3, slab_rows, lattice_z)), f32((bricks * 3 * cap, span_cells))),
        in_specs=[SMEM, SMEM, HBM, VMEM, VMEM, VMEM, VMEM, VMEM, HBM],
        out_specs=(HBM, VMEM),
        scratch_shapes=[
            pltpu.VMEM((3, slab_rows, lattice_z), jnp.float32),
            pltpu.VMEM((3, slab_rows + 2 * NY, lattice_z), jnp.float32),
            pltpu.VMEM((2, 3, NY, lattice_z), jnp.float32),
            pltpu.SemaphoreType.DMA,
        ],
        input_output_aliases={8: 0},
        compiler_params=ROOM,
    )(
        return_row,
        slots,
        spectral,
        edges,
        factors,
        table_y,
        table_z,
        remesh.T,
        advanced.reshape(3, slab_rows, lattice_z),
    )

    returned, index_back = exchange(packed_back, 1)
    fields = pl.pallas_call(
        functools.partial(finish_kernel, cap, stride, bricks),
        out_shape=f32((3, rows_j, NI, span_cells)),
        in_specs=[SMEM, VMEM, HBM, HBM],
        out_specs=HBM,
        scratch_shapes=[
            pltpu.VMEM((3, rows_j, span_cells), jnp.float32),
            pltpu.VMEM((3, rows_j, 8, span_cells), jnp.float32),
            pltpu.VMEM((3, rows_j, 8, span_cells), jnp.float32),
            pltpu.SemaphoreType.DMA((2,)),
        ],
        input_output_aliases={3: 0},
        compiler_params=ROOM,
    )(index_back, returned, near, fields.reshape(3, rows_j, NI, span_cells))
    return fields.reshape(1, 3, cell_count)


def solution(mesh):
    placed = (
        P("grp", None, "dev"),
        P("dev"),
        P(),
        P("dev", None),
        P("dev"),
        P("dev", None),
        P("dev"),
        P("dev"),
    )
    return jax.shard_map(
        on_device, mesh=mesh, in_specs=placed, out_specs=P("grp", None, "dev"), check_vma=False
    )
```
